32 devices in a mesh: row: 8 (over z, y), col: 4 (over x, core).
Axes of the slice: x: 2, y: 2, z: 4, core: 2. Of those that a mesh axis runs over, the one named last changes fastest.
Arguments:
- covariance: float32 [2048, 2048], P('row', 'col')
- courants: float32 [2, 2, 16, 128], replicated, may hold values from -0.9 to 0.9
- process_noise_spread: float32 [16, 128], P('row'), may hold values from 0.1 to 1
- sensor_targets: int32 [128], replicated, may hold values from 0 to 2047, as said below
- noise_variance: float32 [128], replicated, may hold values from 0.2 to 1
Outputs:
- posterior_spread: float32 [2048, 2048], P('row', 'col')
The draws below stay inside these ranges and needn't reach their ends.
Inputs may be any that keep to these rules, and one draw needn't show every extreme that they name: `sensor_targets`: sorted ascending, all distinct; exactly 16 of them lie in each band of 256 consecutive state indices that starts at a multiple of 256.
All inputs are finite; a program needn't handle non-finite values.
Results may differ from the reference program's by a relative error of at most 0.0003.
Values sent between devices are 32-bit elements; how exact they have to be, the bound alone decides.
A program may use at most 64 MiB of HBM per device.

```python
import math
import jax
import jax.numpy as jnp
from jax import lax

NC = 128
ROWS_DEV = 2
OBS_DEV = 16
CYCLES = 2
NR = 16
OBS = 128


def draw_covariance(key, part):
    system_snapshots = NR * NC
    gaussian = jax.random.normal(jax.random.fold_in(key, 11), (system_snapshots, system_snapshots), jnp.float32)
    rough_part = (gaussian + gaussian.T) * (0.4 / math.sqrt(2.0 * system_snapshots))
    variance = jax.random.uniform(jax.random.fold_in(key, 12), (system_snapshots,), jnp.float32, 1.2, 2.4)
    positions = jnp.arange(system_snapshots, dtype=jnp.int32)
    result = rough_part.at[positions, positions].set(variance)
    return result


def draw_sensor_targets(key, part):
    band_cells = ROWS_DEV * NC
    band_total = OBS // OBS_DEV
    band_keys = jax.random.split(jax.random.fold_in(key, 21), band_total)

    def choose(subkey):
        return jnp.sort(jax.random.permutation(subkey, band_cells)[:OBS_DEV].astype(jnp.int32))
    chosen = jax.vmap(choose)(band_keys)
    offsets = jnp.arange(band_total, dtype=jnp.int32)[:, None] * band_cells
    return (chosen + offsets).reshape(OBS).astype(jnp.int32)


def shard_levels(rng, extent, shards, smallest, largest):
    gain, own = 1.0, jax.random.fold_in(rng, 6)
    for axis_at, shards_of in shards:
        heights = jnp.exp(jax.random.uniform(jax.random.fold_in(own, axis_at), (shards_of,), jnp.float32, smallest / len(shards), largest / len(shards)))
        gain = gain * jnp.repeat(heights, extent[axis_at] // shards_of).reshape([-1 if axis == axis_at else 1 for axis in range(len(extent))])
    return gain


def setup_inputs(seed: int = 0) -> dict:
    arg_keys = jax.random.split(jax.random.key(seed), 6)
    return {
        "covariance": draw_covariance(jax.random.fold_in(arg_keys[5], 71), 0),
        "courants": jnp.clip(jax.random.uniform(arg_keys[1], (CYCLES, 2, NR, NC), jnp.float32, -0.9, 0.9), -0.9, 0.9),
        "process_noise_spread": jnp.clip(jnp.exp(math.log(1.0) - 2.3025851 * jax.random.uniform(arg_keys[2], (NR, NC), jnp.float32) ** shard_levels(arg_keys[2], (NR, NC), ((0, 8),), -0.2, 0.2)), 0.1, 1.0),
        "sensor_targets": draw_sensor_targets(jax.random.fold_in(arg_keys[5], 71), 0),
        "noise_variance": jnp.clip(jnp.exp(jax.random.uniform(arg_keys[4], (OBS,), jnp.float32, math.log(0.2), math.log(1.0))), 0.2, 1.0),
    }


finest_accuracy = lax.Precision.HIGHEST

def stencil_weights(courant):
    return (courant * (1.0 + courant) * 0.5, 1.0 - courant * courant, courant * (courant - 1.0) * 0.5)

def sweep_local(joint_spread_array, courant, which_axis):
    weight_behind, weight_centre, weight_ahead = stencil_weights(courant)
    return weight_behind * jnp.roll(joint_spread_array, 1, which_axis) + weight_centre * joint_spread_array + weight_ahead * jnp.roll(joint_spread_array, -1, which_axis)

def reference(covariance, courants, process_noise_spread, sensor_targets, noise_variance):
    system_snapshots = NR * NC
    wrapped_mesh = covariance.reshape(NR, NC, NR, NC)
    for cycle_index in range(CYCLES):
        eastward = courants[cycle_index, 0]
        northward = courants[cycle_index, 1]
        wrapped_mesh = sweep_local(wrapped_mesh, eastward[:, :, None, None], 1)
        wrapped_mesh = sweep_local(wrapped_mesh, northward[:, :, None, None], 0)
        wrapped_mesh = sweep_local(wrapped_mesh, eastward[None, None], 3)
        wrapped_mesh = sweep_local(wrapped_mesh, northward[None, None], 2)
    predicted_spread = wrapped_mesh.reshape(system_snapshots, system_snapshots)
    trace_entry_index = jnp.arange(system_snapshots, dtype=jnp.int32)
    predicted_spread = predicted_spread.at[trace_entry_index, trace_entry_index].add(process_noise_spread.reshape(system_snapshots))
    update_weighting = predicted_spread[:, sensor_targets]
    measured_entries = predicted_spread[sensor_targets, :]
    innovation = measured_entries[:, sensor_targets] + jnp.diag(noise_variance)
    factor = jnp.linalg.cholesky(innovation)
    inverse = jax.scipy.linalg.solve_triangular(factor, jnp.eye(OBS, dtype=jnp.float32), lower=True)
    lower_triangle_source = lax.dot_general(inverse, update_weighting, (((1,), (1,)), ((), ())), precision=finest_accuracy)
    lower_triangle_target = jnp.dot(inverse, measured_entries, precision=finest_accuracy)
    return predicted_spread - lax.dot_general(lower_triangle_source, lower_triangle_target, (((0,), (0,)), ((), ())), precision=finest_accuracy)
```

```python
import functools

import jax
import jax.numpy as jnp
from jax import lax
from jax.experimental import pallas as pl
from jax.experimental.pallas import tpu as pltpu
from jax.sharding import PartitionSpec as P

NC = 128
CYCLES = 2


finest_accuracy = lax.Precision.HIGHEST


def padded_2(array, sides, width):
    for axis, dim in sides:
        size, length = (lax.axis_size(axis), array.shape[dim])
        up = [(i, (i + 1) % size) for i in range(size)]
        down = [(j, i) for i, j in up]
        last = lax.slice_in_dim(array, length - width, length, axis=dim)
        initial = lax.slice_in_dim(array, 0, width, axis=dim)
        before = lax.ppermute(last, axis, up)
        after = lax.ppermute(initial, axis, down)
        array = jnp.concatenate([before, array, after], axis=dim)
    return array


def stencil_weights(courant):
    return (
        courant * (1.0 + courant) * 0.5,
        1.0 - courant * courant,
        courant * (courant - 1.0) * 0.5,
    )


def sweep_local(joint_spread_array, courant, which_axis):
    weight_behind, weight_centre, weight_ahead = stencil_weights(courant)
    return (
        weight_behind * jnp.roll(joint_spread_array, 1, which_axis)
        + weight_centre * joint_spread_array
        + weight_ahead * jnp.roll(joint_spread_array, -1, which_axis)
    )


def sweep_padded(padded, courant, which_axis, keep_rows):
    weight_behind, weight_centre, weight_ahead = stencil_weights(courant)
    lower_rows = lax.slice_in_dim(padded, 0, keep_rows, axis=which_axis)
    middle = lax.slice_in_dim(padded, 1, keep_rows + 1, axis=which_axis)
    upper_rows = lax.slice_in_dim(padded, 2, keep_rows + 2, axis=which_axis)
    return weight_behind * lower_rows + weight_centre * middle + weight_ahead * upper_rows


def wind_rows(courants, cycle_index, component, offset, length):
    surface = courants[cycle_index, component]
    extent_rows = surface.shape[0]
    doubled = jnp.concatenate([surface, surface], axis=0)
    return lax.dynamic_slice_in_dim(doubled, jnp.mod(offset, extent_rows), length, 0)


def gather_kernel(
    row_total, column_total, spread, row_sites, column_sites, gain, rows, innovation,
    gain_all, rows_all, innovation_all,
    gain_send, gain_recv, rows_send, rows_recv, innovation_send, innovation_recv,
):
    row = lax.axis_index("row")
    column = lax.axis_index("col")
    row_share, column_share = row_sites.shape[0], column_sites.shape[0]
    barrier = pltpu.get_barrier_semaphore()
    for step in range(1, column_total):
        peer = lax.rem(column + step, column_total)
        pl.semaphore_signal(barrier, 1, device_id={"col": peer}, device_id_type=pl.DeviceIdType.MESH)
    for step in range(1, row_total):
        peer = lax.rem(row + step, row_total)
        pl.semaphore_signal(barrier, 1, device_id={"row": peer}, device_id_type=pl.DeviceIdType.MESH)

    height, width = spread.shape
    pick_rows = jnp.where(
        row_sites[...] == lax.broadcasted_iota(jnp.int32, (row_share, height), 1), 1.0, 0.0
    )
    pick_columns = jnp.where(
        column_sites[...] == lax.broadcasted_iota(jnp.int32, (column_share, width), 1), 1.0, 0.0
    )

    def gain_block(index):
        return gain_all.at[pl.ds(pl.multiple_of(index * column_share, column_share), column_share)]

    def rows_block(index):
        return rows_all.at[pl.ds(pl.multiple_of(index * row_share, row_share), row_share)]

    def innovation_block(index):
        return innovation_all.at[pl.ds(pl.multiple_of(index * row_share, row_share), row_share)]

    gain_block(column)[...] = lax.dot_general(
        pick_columns, spread[...], (((1,), (1,)), ((), ())),
        precision=finest_accuracy, preferred_element_type=jnp.float32,
    )
    rows_block(row)[...] = jnp.dot(
        pick_rows, spread[...], precision=finest_accuracy, preferred_element_type=jnp.float32
    )
    pl.semaphore_wait(barrier, row_total + column_total - 2)

    def exchange(block, me, axis, total, send, recv):
        copies = []
        for step in range(1, total):
            peer = lax.rem(me + step, total)
            copy = pltpu.make_async_remote_copy(
                src_ref=block(me), dst_ref=block(me),
                send_sem=send.at[step], recv_sem=recv.at[step],
                device_id={axis: peer}, device_id_type=pl.DeviceIdType.MESH,
            )
            copy.start()
            copies.append(copy)
        return copies

    def arrive(block, me, axis, total, send, recv):
        for step in range(1, total):
            source = lax.rem(me - step + total, total)
            pltpu.make_async_remote_copy(
                src_ref=block(source), dst_ref=block(source),
                send_sem=send.at[step], recv_sem=recv.at[step],
                device_id={axis: source}, device_id_type=pl.DeviceIdType.MESH,
            ).wait_recv()

    sent = exchange(gain_block, column, "col", column_total, gain_send, gain_recv)
    sent += exchange(rows_block, row, "row", row_total, rows_send, rows_recv)
    arrive(gain_block, column, "col", column_total, gain_send, gain_recv)
    innovation_block(row)[...] = lax.dot_general(
        pick_rows, gain_all[...], (((1,), (1,)), ((), ())),
        precision=finest_accuracy, preferred_element_type=jnp.float32,
    )
    sent += exchange(innovation_block, row, "row", row_total, innovation_send, innovation_recv)
    gain[...] = gain_all[...]
    arrive(rows_block, row, "row", row_total, rows_send, rows_recv)
    rows[...] = rows_all[...]
    arrive(innovation_block, row, "row", row_total, innovation_send, innovation_recv)
    innovation[...] = innovation_all[...]
    for copy in sent:
        copy.wait_send()


def gather_call(spread, row_sites, column_sites, row_total, column_total):
    height, width = spread.shape
    stations = row_sites.shape[0] * row_total
    shapes = [(stations, height), (stations, width), (stations, stations)]
    vmem = pl.BlockSpec(memory_space=pltpu.VMEM)
    semaphores = [pltpu.SemaphoreType.DMA((column_total,))] * 2
    semaphores += [pltpu.SemaphoreType.DMA((row_total,))] * 4
    return pl.pallas_call(
        functools.partial(gather_kernel, row_total, column_total),
        out_shape=[jax.ShapeDtypeStruct(shape, jnp.float32) for shape in shapes],
        in_specs=[vmem] * 3,
        out_specs=[vmem] * 3,
        scratch_shapes=[pltpu.VMEM(shape, jnp.float32) for shape in shapes] + semaphores,
        compiler_params=pltpu.CompilerParams(
            collective_id=0, has_side_effects=True, vmem_limit_bytes=24 * 2**20
        ),
    )(spread, row_sites[:, None], column_sites[:, None])


PIVOTS = 4


def invert_block(d):
    def mul(x, y):
        return [[x[i][0] * y[0][j] + x[i][1] * y[1][j] for j in range(2)] for i in range(2)]

    def inv(x):
        scale = 1.0 / (x[0][0] * x[1][1] - x[0][1] * x[1][0])
        return [[x[1][1] * scale, -x[0][1] * scale], [-x[1][0] * scale, x[0][0] * scale]]

    def quarter(i, j):
        return [[d[2 * i + a][2 * j + b] for b in range(2)] for a in range(2)]

    def combine(x, y, sign):
        return [[x[i][j] + sign * y[i][j] for j in range(2)] for i in range(2)]

    e, f, g, h = quarter(0, 0), quarter(0, 1), quarter(1, 0), quarter(1, 1)
    ei = inv(e)
    eif, gei = mul(ei, f), mul(g, ei)
    si = inv(combine(h, mul(g, eif), -1.0))
    low = mul(si, gei)
    upper = mul(eif, si)
    first = combine(ei, mul(eif, low), 1.0)
    return [
        first[0] + [-upper[0][0], -upper[0][1]],
        first[1] + [-upper[1][0], -upper[1][1]],
        [-low[0][0], -low[0][1]] + si[0],
        [-low[1][0], -low[1][1]] + si[1],
    ]


def invert(matrix):
    n = matrix.shape[0]
    group = 8
    lanes = lax.broadcasted_iota(jnp.int32, (1, n), 1)
    sublanes = lax.broadcasted_iota(jnp.int32, (group, n), 0)
    parts = [matrix[i : i + group] for i in range(0, n, group)]
    for first in range(0, n, PIVOTS):
        home, at = first // group, first % group
        columns = [
            [jnp.broadcast_to(part[:, first + p : first + p + 1], (group, n)) for p in range(PIVOTS)]
            for part in parts
        ]
        block = [
            [columns[home][p][at + q : at + q + 1] for p in range(PIVOTS)] for q in range(PIVOTS)
        ]
        inverse = invert_block(block)
        outside = jnp.where((lanes >= first) & (lanes < first + PIVOTS), 0.0, 1.0)
        panel = [
            jnp.where(lanes == first + q, 1.0, parts[home][at + q : at + q + 1] * outside)
            for q in range(PIVOTS)
        ]
        solved = [
            sum(inverse[q][p] * panel[p] for p in range(1, PIVOTS)) + inverse[q][0] * panel[0]
            for q in range(PIVOTS)
        ]
        wide = [jnp.broadcast_to(row, (group, n)) for row in solved]
        updated = []
        for i, part in enumerate(parts):
            terms = [columns[i][p] * wide[p] for p in range(PIVOTS)]
            new = part * outside - ((terms[0] + terms[1]) + (terms[2] + terms[3]))
            if i == home:
                for q in range(PIVOTS):
                    new = jnp.where(sublanes == at + q, wide[q], new)
            updated.append(new)
        parts = updated
    return jnp.concatenate(parts, axis=0)


def analysis_kernel(spread, innovation, noise, rows, gain, out):
    stations = innovation.shape[0]
    diagonal = lax.broadcasted_iota(jnp.int32, (stations, stations), 0) == lax.broadcasted_iota(
        jnp.int32, (stations, stations), 1
    )
    matrix = innovation[...]
    matrix = (matrix + matrix.T) * 0.5 + jnp.where(diagonal, noise[...], 0.0)
    inverse = invert(matrix)
    weighted = jnp.dot(
        inverse, rows[...], precision=finest_accuracy, preferred_element_type=jnp.float32
    )
    out[...] = spread[...] - lax.dot_general(
        gain[...], weighted, (((0,), (0,)), ((), ())),
        precision=finest_accuracy, preferred_element_type=jnp.float32,
    )


def analysis_call(spread, innovation, noise, rows, gain):
    stations = innovation.shape[0]
    if stations > NC:
        factor = jnp.linalg.cholesky(innovation + jnp.diag(noise))
        inverse = jax.scipy.linalg.solve_triangular(
            factor, jnp.eye(stations, dtype=jnp.float32), lower=True
        )
        left = jnp.dot(inverse, gain, precision=finest_accuracy)
        right = jnp.dot(inverse, rows, precision=finest_accuracy)
        return spread - lax.dot_general(
            left, right, (((0,), (0,)), ((), ())), precision=finest_accuracy
        )
    vmem = pl.BlockSpec(memory_space=pltpu.VMEM)
    return pl.pallas_call(
        analysis_kernel,
        out_shape=jax.ShapeDtypeStruct(spread.shape, jnp.float32),
        in_specs=[vmem] * 5,
        out_specs=vmem,
        compiler_params=pltpu.CompilerParams(vmem_limit_bytes=24 * 2**20),
    )(spread, innovation, noise[None, :], rows, gain)


def per_device(covariance, courants, process_noise_spread, sensor_targets, noise_variance):
    row_index = lax.axis_index("row")
    column_index = lax.axis_index("col")
    row_total = lax.axis_size("row")
    column_total = lax.axis_size("col")
    horizontal_tile_piece, vertical_tile_piece = covariance.shape
    band_rows = horizontal_tile_piece // NC
    band_columns = vertical_tile_piece // NC
    row_first = row_index * band_rows
    column_first = column_index * band_columns
    joint_spread_array = covariance
    for cycle_index in range(CYCLES):
        joint_spread_array = joint_spread_array.reshape(band_rows, NC, vertical_tile_piece)
        eastward = wind_rows(courants, cycle_index, 0, row_first, band_rows)[:, :, None]
        joint_spread_array = sweep_local(joint_spread_array, eastward, 1)
        padded = padded_2(joint_spread_array, (("row", 0),), 1)
        northward = wind_rows(courants, cycle_index, 1, row_first, band_rows)[:, :, None]
        joint_spread_array = sweep_padded(padded, northward, 0, band_rows)
        joint_spread_array = joint_spread_array.reshape(horizontal_tile_piece, band_columns, NC)
        eastward = wind_rows(courants, cycle_index, 0, column_first, band_columns)[None]
        joint_spread_array = sweep_local(joint_spread_array, eastward, 2)
        padded = padded_2(joint_spread_array, (("col", 1),), 1)
        northward = wind_rows(courants, cycle_index, 1, column_first, band_columns)[None]
        joint_spread_array = sweep_padded(padded, northward, 1, band_columns)
    predicted_spread = joint_spread_array.reshape(horizontal_tile_piece, vertical_tile_piece)
    row_ids = row_index * horizontal_tile_piece + jnp.arange(horizontal_tile_piece, dtype=jnp.int32)
    column_ids = column_index * vertical_tile_piece + jnp.arange(
        vertical_tile_piece, dtype=jnp.int32
    )
    predicted_spread = predicted_spread + jnp.where(
        row_ids[:, None] == column_ids[None, :],
        process_noise_spread.reshape(horizontal_tile_piece, 1),
        0.0,
    )
    station_total = sensor_targets.shape[0]
    row_share = station_total // row_total
    column_share = station_total // column_total
    sensor_horizontal_indices = (
        lax.dynamic_slice_in_dim(sensor_targets, row_index * row_share, row_share)
        - row_index * horizontal_tile_piece
    )
    sensor_vertical_indices = (
        lax.dynamic_slice_in_dim(sensor_targets, column_index * column_share, column_share)
        - column_index * vertical_tile_piece
    )
    gain, rows, innovation = gather_call(
        predicted_spread, sensor_horizontal_indices, sensor_vertical_indices, row_total, column_total
    )
    return analysis_call(predicted_spread, innovation, noise_variance, rows, gain)


def solution(mesh):
    in_specs = (P("row", "col"), P(), P("row", None), P(), P())
    out_specs = P("row", "col")
    return jax.shard_map(
        per_device, mesh=mesh, in_specs=in_specs, out_specs=out_specs, check_vma=False
    )
```

```python
import functools

import jax
import jax.numpy as jnp
from jax import lax
from jax.experimental import pallas as pl
from jax.experimental.pallas import tpu as pltpu
from jax.sharding import PartitionSpec as P

NC = 128
CYCLES = 2


finest_accuracy = lax.Precision.HIGHEST


def sweep(behind, centre, ahead, courant):
    total = None
    for value, weight in (
        (behind, lambda: courant * (1.0 + courant) * 0.5),
        (centre, lambda: 1.0 - courant * courant),
        (ahead, lambda: courant * (courant - 1.0) * 0.5),
    ):
        if value is not None:
            term = weight() * value
            total = term if total is None else total + term
    return total


def advance(stack, winds, axis):
    length = NC
    for cycle in range(CYCLES):
        stack = [
            None if line is None else sweep(
                pltpu.roll(line, 1, axis), line, pltpu.roll(line, length - 1, axis),
                winds(cycle, 0, cycle + at),
            )
            for at, line in enumerate(stack)
        ]
        stack = [
            sweep(stack[at - 1], stack[at], stack[at + 1], winds(cycle, 1, cycle + at))
            for at in range(1, len(stack) - 1)
        ]
    return stack


def forecast_kernel(
    row_total, column_total, covariance, courants, noise, out,
    wind, done, travelled, term, arrived, behind, ahead,
    far_send, far_recv, near_send, near_recv, behind_send, behind_recv, ahead_send, ahead_recv,
):
    row = lax.axis_index("row")
    column = lax.axis_index("col")
    height, width = covariance.shape
    band_rows, band_columns = height // NC, width // NC
    grid_rows = courants.shape[2]
    half = lax.rem(row, 2)
    partner = row + 1 - 2 * half
    far_target = lax.rem(row + 4 * half - 2 + row_total, row_total)
    far_source = lax.rem(row + 2 - 4 * half + row_total, row_total)
    before = lax.rem(column + column_total - 1, column_total)
    after = lax.rem(column + 1, column_total)
    mesh_id = pl.DeviceIdType.MESH

    barrier = pltpu.get_barrier_semaphore()
    for peer in (far_target, far_source, partner):
        pl.semaphore_signal(barrier, 1, device_id={"row": peer}, device_id_type=mesh_id)
    for peer in (before, after):
        pl.semaphore_signal(barrier, 1, device_id={"col": peer}, device_id_type=mesh_id)
    pl.semaphore_wait(barrier, 5)

    def chunk(k):
        return covariance.at[:, k * NC : (k + 1) * NC]

    def copy(source, target, send, recv, at, axis, peer):
        return pltpu.make_async_remote_copy(
            src_ref=source, dst_ref=target, send_sem=send.at[at], recv_sem=recv.at[at],
            device_id={axis: peer}, device_id_type=mesh_id,
        )

    far = [
        copy(chunk(k), travelled.at[k], far_send, far_recv, k, "row", far_target)
        for k in range(band_columns)
    ]
    for transfer in far:
        transfer.start()

    window = 2 * band_rows + 2 * CYCLES
    pair_first = (row - half) * band_rows - CYCLES + grid_rows
    for cycle in range(CYCLES):
        for component in range(2):
            for at in range(window):
                line = courants[
                    cycle, component, pl.ds(lax.rem(pair_first + at, grid_rows), 1), :
                ]
                wind[cycle, component, at] = jnp.broadcast_to(line, (NC, NC)).T

    def winds_of(offset):
        return lambda cycle, component, at: wind[cycle, component, offset + at]

    own_offset = half * band_rows
    other_offset = band_rows - own_offset

    def own_part(k, _):
        columns = pl.ds(pl.multiple_of(k * NC, NC), NC)
        own = [covariance[i * NC : (i + 1) * NC, columns] for i in range(band_rows)]
        lines = advance([None] * CYCLES + own + [None] * CYCLES, winds_of(own_offset), 0)
        for i, line in enumerate(lines):
            done[k, i * NC : (i + 1) * NC, :] = line
        return 0

    lax.fori_loop(0, band_columns, own_part, 0)

    near = [
        copy(term.at[k], arrived.at[k], near_send, near_recv, k, "row", partner)
        for k in range(band_columns)
    ]
    sides = []

    def finish(k):
        near[k].wait_recv()
        done[k] = done[k] + arrived[k]
        if k < CYCLES:
            sides.append(copy(done.at[k], ahead.at[k], ahead_send, ahead_recv, k, "col", before))
            sides[-1].start()
        if k >= band_columns - CYCLES:
            at = k - (band_columns - CYCLES)
            sides.append(copy(done.at[k], behind.at[at], behind_send, behind_recv, at, "col", after))
            sides[-1].start()

    for k in range(band_columns):
        far[k].wait_recv()
        lower, upper = [], []
        for i in range(band_rows):
            rows = slice(i * NC, (i + 1) * NC)
            own, other = covariance[rows, k * NC : (k + 1) * NC], travelled[k, rows, :]
            lower.append(jnp.where(half == 1, other, own))
            upper.append(jnp.where(half == 1, own, other))
        lines = advance(lower + [None] * band_rows + upper, winds_of(other_offset), 0)
        for i, line in enumerate(lines):
            term[k, i * NC : (i + 1) * NC, :] = line
        near[k].start()
        if k:
            finish(k - 1)
    finish(band_columns - 1)
    for transfer in sides:
        transfer.wait_recv()

    column_first = column * band_columns - CYCLES + grid_rows
    column_winds = {
        (cycle, component, at): courants[
            cycle, component, pl.ds(lax.rem(column_first + at, grid_rows), 1), :
        ]
        for cycle in range(CYCLES)
        for component in range(2)
        for at in range(band_columns + 2 * CYCLES)
    }
    step = 32
    for i in range(band_rows):
        cell_noise = noise[i : i + 1, :]

        def piece(m, _):
            first = pl.multiple_of(m * step, step)
            rows = pl.ds(i * NC + first, step)
            stack = [behind[k, rows, :] for k in range(CYCLES)]
            stack += [done[k, rows, :] for k in range(band_columns)]
            stack += [ahead[k, rows, :] for k in range(CYCLES)]
            lines = advance(stack, lambda *key: column_winds[key], 1)
            matches = first + lax.broadcasted_iota(
                jnp.int32, (step, NC), 0
            ) == lax.broadcasted_iota(jnp.int32, (step, NC), 1)
            for k, line in enumerate(lines):
                here = row * band_rows + i == column * band_columns + k
                extra = jnp.where(matches & here, cell_noise, 0.0)
                out[rows, k * NC : (k + 1) * NC] = line + extra
            return 0

        lax.fori_loop(0, NC // step, piece, 0)

    for transfer in far + near + sides:
        transfer.wait_send()


def forecast_call(covariance, courants, noise, row_total, column_total):
    height, width = covariance.shape
    band_rows, band_columns = height // NC, width // NC
    vmem = pl.BlockSpec(memory_space=pltpu.VMEM)
    lines = pltpu.VMEM((band_columns, height, NC), jnp.float32)
    side = pltpu.VMEM((CYCLES, height, NC), jnp.float32)
    window = 2 * band_rows + 2 * CYCLES
    return pl.pallas_call(
        functools.partial(forecast_kernel, row_total, column_total),
        out_shape=jax.ShapeDtypeStruct(covariance.shape, jnp.float32),
        in_specs=[vmem] * 3,
        out_specs=vmem,
        scratch_shapes=[pltpu.VMEM((CYCLES, 2, window, NC, NC), jnp.float32)]
        + [lines] * 4
        + [side] * 2
        + [pltpu.SemaphoreType.DMA((band_columns,))] * 4
        + [pltpu.SemaphoreType.DMA((CYCLES,))] * 4,
        compiler_params=pltpu.CompilerParams(
            collective_id=1, has_side_effects=True, vmem_limit_bytes=24 * 2**20
        ),
    )(covariance, courants, noise)


def gather_kernel(
    row_total, column_total, spread, row_sites, column_sites, gain, rows, innovation,
    gain_all, rows_all, innovation_all,
    gain_send, gain_recv, rows_send, rows_recv, innovation_send, innovation_recv,
):
    row = lax.axis_index("row")
    column = lax.axis_index("col")
    row_share, column_share = row_sites.shape[0], column_sites.shape[0]
    barrier = pltpu.get_barrier_semaphore()
    for step in range(1, column_total):
        peer = lax.rem(column + step, column_total)
        pl.semaphore_signal(barrier, 1, device_id={"col": peer}, device_id_type=pl.DeviceIdType.MESH)
    for step in range(1, row_total):
        peer = lax.rem(row + step, row_total)
        pl.semaphore_signal(barrier, 1, device_id={"row": peer}, device_id_type=pl.DeviceIdType.MESH)

    height, width = spread.shape
    pick_rows = jnp.where(
        row_sites[...] == lax.broadcasted_iota(jnp.int32, (row_share, height), 1), 1.0, 0.0
    )
    pick_columns = jnp.where(
        column_sites[...] == lax.broadcasted_iota(jnp.int32, (column_share, width), 1), 1.0, 0.0
    )

    def gain_block(index):
        return gain_all.at[pl.ds(pl.multiple_of(index * column_share, column_share), column_share)]

    def rows_block(index):
        return rows_all.at[pl.ds(pl.multiple_of(index * row_share, row_share), row_share)]

    def innovation_block(index):
        return innovation_all.at[pl.ds(pl.multiple_of(index * row_share, row_share), row_share)]

    gain_block(column)[...] = lax.dot_general(
        pick_columns, spread[...], (((1,), (1,)), ((), ())),
        precision=finest_accuracy, preferred_element_type=jnp.float32,
    )
    rows_block(row)[...] = jnp.dot(
        pick_rows, spread[...], precision=finest_accuracy, preferred_element_type=jnp.float32
    )
    pl.semaphore_wait(barrier, row_total + column_total - 2)

    def exchange(block, me, axis, total, send, recv):
        copies = []
        for step in range(1, total):
            peer = lax.rem(me + step, total)
            copy = pltpu.make_async_remote_copy(
                src_ref=block(me), dst_ref=block(me),
                send_sem=send.at[step], recv_sem=recv.at[step],
                device_id={axis: peer}, device_id_type=pl.DeviceIdType.MESH,
            )
            copy.start()
            copies.append(copy)
        return copies

    def arrive(block, me, axis, total, send, recv):
        for step in range(1, total):
            source = lax.rem(me - step + total, total)
            pltpu.make_async_remote_copy(
                src_ref=block(source), dst_ref=block(source),
                send_sem=send.at[step], recv_sem=recv.at[step],
                device_id={axis: source}, device_id_type=pl.DeviceIdType.MESH,
            ).wait_recv()

    sent = exchange(gain_block, column, "col", column_total, gain_send, gain_recv)
    sent += exchange(rows_block, row, "row", row_total, rows_send, rows_recv)
    arrive(gain_block, column, "col", column_total, gain_send, gain_recv)
    innovation_block(row)[...] = lax.dot_general(
        pick_rows, gain_all[...], (((1,), (1,)), ((), ())),
        precision=finest_accuracy, preferred_element_type=jnp.float32,
    )
    sent += exchange(innovation_block, row, "row", row_total, innovation_send, innovation_recv)
    gain[...] = gain_all[...]
    arrive(rows_block, row, "row", row_total, rows_send, rows_recv)
    rows[...] = rows_all[...]
    arrive(innovation_block, row, "row", row_total, innovation_send, innovation_recv)
    innovation[...] = innovation_all[...]
    for copy in sent:
        copy.wait_send()


def gather_call(spread, row_sites, column_sites, row_total, column_total):
    height, width = spread.shape
    stations = row_sites.shape[0] * row_total
    shapes = [(stations, height), (stations, width), (stations, stations)]
    vmem = pl.BlockSpec(memory_space=pltpu.VMEM)
    semaphores = [pltpu.SemaphoreType.DMA((column_total,))] * 2
    semaphores += [pltpu.SemaphoreType.DMA((row_total,))] * 4
    return pl.pallas_call(
        functools.partial(gather_kernel, row_total, column_total),
        out_shape=[jax.ShapeDtypeStruct(shape, jnp.float32) for shape in shapes],
        in_specs=[vmem] * 3,
        out_specs=[vmem] * 3,
        scratch_shapes=[pltpu.VMEM(shape, jnp.float32) for shape in shapes] + semaphores,
        compiler_params=pltpu.CompilerParams(
            collective_id=0, has_side_effects=True, vmem_limit_bytes=24 * 2**20
        ),
    )(spread, row_sites[:, None], column_sites[:, None])


PIVOTS = 4


def invert_block(d):
    def mul(x, y):
        return [[x[i][0] * y[0][j] + x[i][1] * y[1][j] for j in range(2)] for i in range(2)]

    def inv(x):
        scale = 1.0 / (x[0][0] * x[1][1] - x[0][1] * x[1][0])
        return [[x[1][1] * scale, -x[0][1] * scale], [-x[1][0] * scale, x[0][0] * scale]]

    def quarter(i, j):
        return [[d[2 * i + a][2 * j + b] for b in range(2)] for a in range(2)]

    def combine(x, y, sign):
        return [[x[i][j] + sign * y[i][j] for j in range(2)] for i in range(2)]

    e, f, g, h = quarter(0, 0), quarter(0, 1), quarter(1, 0), quarter(1, 1)
    ei = inv(e)
    eif, gei = mul(ei, f), mul(g, ei)
    si = inv(combine(h, mul(g, eif), -1.0))
    low = mul(si, gei)
    upper = mul(eif, si)
    first = combine(ei, mul(eif, low), 1.0)
    return [
        first[0] + [-upper[0][0], -upper[0][1]],
        first[1] + [-upper[1][0], -upper[1][1]],
        [-low[0][0], -low[0][1]] + si[0],
        [-low[1][0], -low[1][1]] + si[1],
    ]


def invert(matrix):
    n = matrix.shape[0]
    group = 8
    lanes = lax.broadcasted_iota(jnp.int32, (1, n), 1)
    sublanes = lax.broadcasted_iota(jnp.int32, (group, n), 0)
    parts = [matrix[i : i + group] for i in range(0, n, group)]
    for first in range(0, n, PIVOTS):
        home, at = first // group, first % group
        columns = [
            [jnp.broadcast_to(part[:, first + p : first + p + 1], (group, n)) for p in range(PIVOTS)]
            for part in parts
        ]
        block = [
            [columns[home][p][at + q : at + q + 1] for p in range(PIVOTS)] for q in range(PIVOTS)
        ]
        inverse = invert_block(block)
        outside = jnp.where((lanes >= first) & (lanes < first + PIVOTS), 0.0, 1.0)
        panel = [
            jnp.where(lanes == first + q, 1.0, parts[home][at + q : at + q + 1] * outside)
            for q in range(PIVOTS)
        ]
        solved = [
            sum(inverse[q][p] * panel[p] for p in range(1, PIVOTS)) + inverse[q][0] * panel[0]
            for q in range(PIVOTS)
        ]
        wide = [jnp.broadcast_to(row, (group, n)) for row in solved]
        updated = []
        for i, part in enumerate(parts):
            terms = [columns[i][p] * wide[p] for p in range(PIVOTS)]
            new = part * outside - ((terms[0] + terms[1]) + (terms[2] + terms[3]))
            if i == home:
                for q in range(PIVOTS):
                    new = jnp.where(sublanes == at + q, wide[q], new)
            updated.append(new)
        parts = updated
    return jnp.concatenate(parts, axis=0)


def analysis_kernel(spread, innovation, noise, rows, gain, out):
    stations = innovation.shape[0]
    diagonal = lax.broadcasted_iota(jnp.int32, (stations, stations), 0) == lax.broadcasted_iota(
        jnp.int32, (stations, stations), 1
    )
    matrix = innovation[...]
    matrix = (matrix + matrix.T) * 0.5 + jnp.where(diagonal, noise[...], 0.0)
    inverse = invert(matrix)
    weighted = jnp.dot(
        inverse, rows[...], precision=finest_accuracy, preferred_element_type=jnp.float32
    )
    out[...] = spread[...] - lax.dot_general(
        gain[...], weighted, (((0,), (0,)), ((), ())),
        precision=finest_accuracy, preferred_element_type=jnp.float32,
    )


def analysis_call(spread, innovation, noise, rows, gain):
    stations = innovation.shape[0]
    if stations > NC:
        factor = jnp.linalg.cholesky(innovation + jnp.diag(noise))
        inverse = jax.scipy.linalg.solve_triangular(
            factor, jnp.eye(stations, dtype=jnp.float32), lower=True
        )
        left = jnp.dot(inverse, gain, precision=finest_accuracy)
        right = jnp.dot(inverse, rows, precision=finest_accuracy)
        return spread - lax.dot_general(
            left, right, (((0,), (0,)), ((), ())), precision=finest_accuracy
        )
    vmem = pl.BlockSpec(memory_space=pltpu.VMEM)
    return pl.pallas_call(
        analysis_kernel,
        out_shape=jax.ShapeDtypeStruct(spread.shape, jnp.float32),
        in_specs=[vmem] * 5,
        out_specs=vmem,
        compiler_params=pltpu.CompilerParams(vmem_limit_bytes=24 * 2**20),
    )(spread, innovation, noise[None, :], rows, gain)


def per_device(covariance, courants, process_noise_spread, sensor_targets, noise_variance):
    row_index = lax.axis_index("row")
    column_index = lax.axis_index("col")
    row_total = lax.axis_size("row")
    column_total = lax.axis_size("col")
    horizontal_tile_piece, vertical_tile_piece = covariance.shape
    predicted_spread = forecast_call(
        covariance, courants, process_noise_spread, row_total, column_total
    )
    station_total = sensor_targets.shape[0]
    row_share = station_total // row_total
    column_share = station_total // column_total
    sensor_horizontal_indices = (
        lax.dynamic_slice_in_dim(sensor_targets, row_index * row_share, row_share)
        - row_index * horizontal_tile_piece
    )
    sensor_vertical_indices = (
        lax.dynamic_slice_in_dim(sensor_targets, column_index * column_share, column_share)
        - column_index * vertical_tile_piece
    )
    gain, rows, innovation = gather_call(
        predicted_spread, sensor_horizontal_indices, sensor_vertical_indices, row_total, column_total
    )
    return analysis_call(predicted_spread, innovation, noise_variance, rows, gain)


def solution(mesh):
    in_specs = (P("row", "col"), P(), P("row", None), P(), P())
    out_specs = P("row", "col")
    return jax.shard_map(
        per_device, mesh=mesh, in_specs=in_specs, out_specs=out_specs, check_vma=False
    )
```

```python
import functools

import jax
import jax.numpy as jnp
from jax import lax
from jax.experimental import pallas as pl
from jax.experimental.pallas import tpu as pltpu
from jax.sharding import PartitionSpec as P

NC = 128
CYCLES = 2


finest_accuracy = lax.Precision.HIGHEST


def sweep(behind, centre, ahead, courant):
    total = None
    for value, weight in (
        (behind, lambda: courant * (1.0 + courant) * 0.5),
        (centre, lambda: 1.0 - courant * courant),
        (ahead, lambda: courant * (courant - 1.0) * 0.5),
    ):
        if value is not None:
            term = weight() * value
            total = term if total is None else total + term
    return total


def advance(stack, winds, axis):
    length = NC
    for cycle in range(CYCLES):
        stack = [
            None if line is None else sweep(
                pltpu.roll(line, 1, axis), line, pltpu.roll(line, length - 1, axis),
                winds(cycle, 0, cycle + at),
            )
            for at, line in enumerate(stack)
        ]
        stack = [
            sweep(stack[at - 1], stack[at], stack[at + 1], winds(cycle, 1, cycle + at))
            for at in range(1, len(stack) - 1)
        ]
    return stack


def forecast_kernel(
    row_total, column_total, covariance_in, courants_in, noise_in, targets_in, variance_in,
    out, gain_out, rows_out, innovation_out,
    covariance, courants, noise, targets, variance, sites, gain_all, rows_all, innovation_all,
    wind, done, travelled, term, arrived, behind, ahead, load,
    far_send, far_recv, near_send, near_recv, behind_send, behind_recv, ahead_send, ahead_recv,
    gain_send, gain_recv, rows_send, rows_recv, innovation_send, innovation_recv,
):
    row = lax.axis_index("row")
    column = lax.axis_index("col")
    height, width = covariance.shape
    band_rows, band_columns = height // NC, width // NC
    grid_rows = courants.shape[2]
    half = lax.rem(row, 2)
    partner = row + 1 - 2 * half
    far_target = lax.rem(row + 4 * half - 2 + row_total, row_total)
    far_source = lax.rem(row + 2 - 4 * half + row_total, row_total)
    before = lax.rem(column + column_total - 1, column_total)
    after = lax.rem(column + 1, column_total)
    mesh_id = pl.DeviceIdType.MESH

    loads = [
        pltpu.make_async_copy(source, target, load.at[at])
        for at, (source, target) in enumerate(
            ((covariance_in, covariance), (courants_in, courants), (noise_in, noise),
             (targets_in, targets), (variance_in, variance))
        )
    ]
    for transfer in loads:
        transfer.start()
    barrier = pltpu.get_barrier_semaphore()
    for step in range(1, column_total):
        peer = lax.rem(column + step, column_total)
        pl.semaphore_signal(barrier, 1, device_id={"col": peer}, device_id_type=mesh_id)
    for step in range(1, row_total):
        peer = lax.rem(row + step, row_total)
        pl.semaphore_signal(barrier, 1, device_id={"row": peer}, device_id_type=mesh_id)
    for transfer in loads:
        transfer.wait()
    pl.semaphore_wait(barrier, row_total + column_total - 2)

    def chunk(k):
        return covariance.at[:, k * NC : (k + 1) * NC]

    def copy(source, target, send, recv, at, axis, peer):
        return pltpu.make_async_remote_copy(
            src_ref=source, dst_ref=target, send_sem=send.at[at], recv_sem=recv.at[at],
            device_id={axis: peer}, device_id_type=mesh_id,
        )

    far = [
        copy(chunk(k), travelled.at[k], far_send, far_recv, k, "row", far_target)
        for k in range(band_columns)
    ]
    for transfer in far:
        transfer.start()

    stations = targets.shape[1]
    row_share, column_share = stations // row_total, stations // column_total
    sites[...] = jnp.broadcast_to(targets[...], (NC, stations)).T

    window = 2 * band_rows + 2 * CYCLES
    pair_first = (row - half) * band_rows - CYCLES + grid_rows
    for cycle in range(CYCLES):
        for component in range(2):
            for at in range(window):
                line = courants[
                    cycle, component, pl.ds(lax.rem(pair_first + at, grid_rows), 1), :
                ]
                wind[cycle, component, at] = jnp.broadcast_to(line, (NC, NC)).T

    def winds_of(offset):
        return lambda cycle, component, at: wind[cycle, component, offset + at]

    own_offset = half * band_rows
    other_offset = band_rows - own_offset

    def own_part(k, _):
        columns = pl.ds(pl.multiple_of(k * NC, NC), NC)
        own = [covariance[i * NC : (i + 1) * NC, columns] for i in range(band_rows)]
        lines = advance([None] * CYCLES + own + [None] * CYCLES, winds_of(own_offset), 0)
        for i, line in enumerate(lines):
            done[k, i * NC : (i + 1) * NC, :] = line
        return 0

    lax.fori_loop(0, band_columns, own_part, 0)

    near = [
        copy(term.at[k], arrived.at[k], near_send, near_recv, k, "row", partner)
        for k in range(band_columns)
    ]
    sides = []

    def finish(k):
        near[k].wait_recv()
        done[k] = done[k] + arrived[k]
        if k < CYCLES:
            sides.append(copy(done.at[k], ahead.at[k], ahead_send, ahead_recv, k, "col", before))
            sides[-1].start()
        if k >= band_columns - CYCLES:
            at = k - (band_columns - CYCLES)
            sides.append(copy(done.at[k], behind.at[at], behind_send, behind_recv, at, "col", after))
            sides[-1].start()

    for k in range(band_columns):
        far[k].wait_recv()
        lower, upper = [], []
        for i in range(band_rows):
            rows = slice(i * NC, (i + 1) * NC)
            own, other = covariance[rows, k * NC : (k + 1) * NC], travelled[k, rows, :]
            lower.append(jnp.where(half == 1, other, own))
            upper.append(jnp.where(half == 1, own, other))
        lines = advance(lower + [None] * band_rows + upper, winds_of(other_offset), 0)
        for i, line in enumerate(lines):
            term[k, i * NC : (i + 1) * NC, :] = line
        near[k].start()
        if k:
            finish(k - 1)
    finish(band_columns - 1)
    for transfer in sides:
        transfer.wait_recv()

    column_first = column * band_columns - CYCLES + grid_rows
    column_winds = {
        (cycle, component, at): courants[
            cycle, component, pl.ds(lax.rem(column_first + at, grid_rows), 1), :
        ]
        for cycle in range(CYCLES)
        for component in range(2)
        for at in range(band_columns + 2 * CYCLES)
    }
    step = 32
    for i in range(band_rows):
        cell_noise = noise[i : i + 1, :]

        def piece(m, _):
            first = pl.multiple_of(m * step, step)
            rows = pl.ds(i * NC + first, step)
            stack = [behind[k, rows, :] for k in range(CYCLES)]
            stack += [done[k, rows, :] for k in range(band_columns)]
            stack += [ahead[k, rows, :] for k in range(CYCLES)]
            lines = advance(stack, lambda *key: column_winds[key], 1)
            matches = first + lax.broadcasted_iota(
                jnp.int32, (step, NC), 0
            ) == lax.broadcasted_iota(jnp.int32, (step, NC), 1)
            for k, line in enumerate(lines):
                here = row * band_rows + i == column * band_columns + k
                extra = jnp.where(matches & here, cell_noise, 0.0)
                out[rows, k * NC : (k + 1) * NC] = line + extra
            return 0

        lax.fori_loop(0, NC // step, piece, 0)

    def picks(share, index, extent):
        first = pl.multiple_of(index * share, share)
        local = sites[pl.ds(first, share), :] - index * extent
        lanes = lax.broadcasted_iota(jnp.int32, (share, NC), 1)
        return jnp.concatenate(
            [jnp.where(local == lanes + at, 1.0, 0.0) for at in range(0, extent, NC)], axis=1
        )

    pick_rows = picks(row_share, row, height)
    pick_columns = picks(column_share, column, width)

    def gain_block(index):
        return gain_all.at[pl.ds(pl.multiple_of(index * column_share, column_share), column_share)]

    def rows_block(index):
        return rows_all.at[pl.ds(pl.multiple_of(index * row_share, row_share), row_share)]

    def innovation_block(index):
        return innovation_all.at[pl.ds(pl.multiple_of(index * row_share, row_share), row_share)]

    gain_block(column)[...] = lax.dot_general(
        pick_columns, out[...], (((1,), (1,)), ((), ())),
        precision=finest_accuracy, preferred_element_type=jnp.float32,
    )
    rows_block(row)[...] = jnp.dot(
        pick_rows, out[...], precision=finest_accuracy, preferred_element_type=jnp.float32
    )

    def exchange(block, me, axis, total, send, recv):
        copies = []
        for step in range(1, total):
            peer = lax.rem(me + step, total)
            transfer = pltpu.make_async_remote_copy(
                src_ref=block(me), dst_ref=block(me),
                send_sem=send.at[step], recv_sem=recv.at[step],
                device_id={axis: peer}, device_id_type=pl.DeviceIdType.MESH,
            )
            transfer.start()
            copies.append(transfer)
        return copies

    def arrive(block, me, axis, total, send, recv):
        for step in range(1, total):
            source = lax.rem(me - step + total, total)
            pltpu.make_async_remote_copy(
                src_ref=block(source), dst_ref=block(source),
                send_sem=send.at[step], recv_sem=recv.at[step],
                device_id={axis: source}, device_id_type=pl.DeviceIdType.MESH,
            ).wait_recv()

    sent = exchange(gain_block, column, "col", column_total, gain_send, gain_recv)
    sent += exchange(rows_block, row, "row", row_total, rows_send, rows_recv)
    arrive(gain_block, column, "col", column_total, gain_send, gain_recv)
    innovation_block(row)[...] = lax.dot_general(
        pick_rows, gain_all[...], (((1,), (1,)), ((), ())),
        precision=finest_accuracy, preferred_element_type=jnp.float32,
    )
    sent += exchange(innovation_block, row, "row", row_total, innovation_send, innovation_recv)
    gain_out[...] = gain_all[...]
    arrive(rows_block, row, "row", row_total, rows_send, rows_recv)
    rows_out[...] = rows_all[...]
    arrive(innovation_block, row, "row", row_total, innovation_send, innovation_recv)
    square = (stations, stations)
    diagonal = lax.broadcasted_iota(jnp.int32, square, 0) == lax.broadcasted_iota(
        jnp.int32, square, 1
    )
    innovation_out[...] = innovation_all[...] + jnp.where(diagonal, variance[...], 0.0)
    for transfer in far + near + sides + sent:
        transfer.wait_send()


def forecast_call(covariance, courants, noise, targets, variance, row_total, column_total):
    height, width = covariance.shape
    stations = targets.shape[0]
    band_rows, band_columns = height // NC, width // NC
    vmem = pl.BlockSpec(memory_space=pltpu.VMEM)
    lines = pltpu.VMEM((band_columns, height, NC), jnp.float32)
    side = pltpu.VMEM((CYCLES, height, NC), jnp.float32)
    window = 2 * band_rows + 2 * CYCLES
    shapes = [(stations, height), (stations, width), (stations, stations)]
    return pl.pallas_call(
        functools.partial(forecast_kernel, row_total, column_total),
        out_shape=[
            jax.ShapeDtypeStruct(shape, jnp.float32) for shape in [covariance.shape] + shapes
        ],
        in_specs=[pl.BlockSpec(memory_space=pltpu.HBM)] * 5,
        out_specs=[vmem] * 4,
        scratch_shapes=[
            pltpu.VMEM(covariance.shape, jnp.float32),
            pltpu.VMEM(courants.shape, jnp.float32),
            pltpu.VMEM(noise.shape, jnp.float32),
            pltpu.VMEM((1, stations), jnp.int32),
            pltpu.VMEM((1, stations), jnp.float32),
            pltpu.VMEM((stations, NC), jnp.int32),
        ]
        + [pltpu.VMEM(shape, jnp.float32) for shape in shapes]
        + [pltpu.VMEM((CYCLES, 2, window, NC, NC), jnp.float32)]
        + [lines] * 4
        + [side] * 2
        + [pltpu.SemaphoreType.DMA((5,))]
        + [pltpu.SemaphoreType.DMA((band_columns,))] * 4
        + [pltpu.SemaphoreType.DMA((CYCLES,))] * 4
        + [pltpu.SemaphoreType.DMA((column_total,))] * 2
        + [pltpu.SemaphoreType.DMA((row_total,))] * 4,
        compiler_params=pltpu.CompilerParams(
            collective_id=0, has_side_effects=True, vmem_limit_bytes=40 * 2**20
        ),
    )(covariance, courants, noise, targets[None, :], variance[None, :])


PIVOTS = 4


def invert_block(d):
    def mul(x, y):
        return [[x[i][0] * y[0][j] + x[i][1] * y[1][j] for j in range(2)] for i in range(2)]

    def inv(x):
        scale = 1.0 / (x[0][0] * x[1][1] - x[0][1] * x[1][0])
        return [[x[1][1] * scale, -x[0][1] * scale], [-x[1][0] * scale, x[0][0] * scale]]

    def quarter(i, j):
        return [[d[2 * i + a][2 * j + b] for b in range(2)] for a in range(2)]

    def combine(x, y, sign):
        return [[x[i][j] + sign * y[i][j] for j in range(2)] for i in range(2)]

    e, f, g, h = quarter(0, 0), quarter(0, 1), quarter(1, 0), quarter(1, 1)
    ei = inv(e)
    eif, gei = mul(ei, f), mul(g, ei)
    si = inv(combine(h, mul(g, eif), -1.0))
    low = mul(si, gei)
    upper = mul(eif, si)
    first = combine(ei, mul(eif, low), 1.0)
    return [
        first[0] + [-upper[0][0], -upper[0][1]],
        first[1] + [-upper[1][0], -upper[1][1]],
        [-low[0][0], -low[0][1]] + si[0],
        [-low[1][0], -low[1][1]] + si[1],
    ]


def invert(matrix):
    n = matrix.shape[0]
    group = 8
    lanes = lax.broadcasted_iota(jnp.int32, (1, n), 1)
    sublanes = lax.broadcasted_iota(jnp.int32, (group, n), 0)
    parts = [matrix[i : i + group] for i in range(0, n, group)]
    for first in range(0, n, PIVOTS):
        home, at = first // group, first % group
        columns = [
            [jnp.broadcast_to(part[:, first + p : first + p + 1], (group, n)) for p in range(PIVOTS)]
            for part in parts
        ]
        block = [
            [columns[home][p][at + q : at + q + 1] for p in range(PIVOTS)] for q in range(PIVOTS)
        ]
        inverse = invert_block(block)
        outside = jnp.where((lanes >= first) & (lanes < first + PIVOTS), 0.0, 1.0)
        panel = [
            jnp.where(lanes == first + q, 1.0, parts[home][at + q : at + q + 1] * outside)
            for q in range(PIVOTS)
        ]
        solved = [
            sum(inverse[q][p] * panel[p] for p in range(1, PIVOTS)) + inverse[q][0] * panel[0]
            for q in range(PIVOTS)
        ]
        wide = [jnp.broadcast_to(row, (group, n)) for row in solved]
        updated = []
        for i, part in enumerate(parts):
            terms = [columns[i][p] * wide[p] for p in range(PIVOTS)]
            new = part * outside - ((terms[0] + terms[1]) + (terms[2] + terms[3]))
            if i == home:
                for q in range(PIVOTS):
                    new = jnp.where(sublanes == at + q, wide[q], new)
            updated.append(new)
        parts = updated
    return jnp.concatenate(parts, axis=0)


def analysis_kernel(spread, innovation, rows, gain, out):
    matrix = innovation[...]
    matrix = (matrix + matrix.T) * 0.5
    inverse = invert(matrix)
    weighted = jnp.dot(
        inverse, rows[...], precision=finest_accuracy, preferred_element_type=jnp.float32
    )
    out[...] = spread[...] - lax.dot_general(
        gain[...], weighted, (((0,), (0,)), ((), ())),
        precision=finest_accuracy, preferred_element_type=jnp.float32,
    )


def analysis_call(spread, innovation, rows, gain):
    stations = innovation.shape[0]
    if stations > NC:
        factor = jnp.linalg.cholesky(innovation)
        inverse = jax.scipy.linalg.solve_triangular(
            factor, jnp.eye(stations, dtype=jnp.float32), lower=True
        )
        left = jnp.dot(inverse, gain, precision=finest_accuracy)
        right = jnp.dot(inverse, rows, precision=finest_accuracy)
        return spread - lax.dot_general(
            left, right, (((0,), (0,)), ((), ())), precision=finest_accuracy
        )
    vmem = pl.BlockSpec(memory_space=pltpu.VMEM)
    return pl.pallas_call(
        analysis_kernel,
        out_shape=jax.ShapeDtypeStruct(spread.shape, jnp.float32),
        in_specs=[vmem] * 4,
        out_specs=vmem,
        compiler_params=pltpu.CompilerParams(vmem_limit_bytes=24 * 2**20),
    )(spread, innovation, rows, gain)


def per_device(covariance, courants, process_noise_spread, sensor_targets, noise_variance):
    spread, gain, rows, innovation = forecast_call(
        covariance, courants, process_noise_spread, sensor_targets, noise_variance,
        lax.axis_size("row"), lax.axis_size("col"),
    )
    return analysis_call(spread, innovation, rows, gain)


def solution(mesh):
    in_specs = (P("row", "col"), P(), P("row", None), P(), P())
    out_specs = P("row", "col")
    return jax.shard_map(
        per_device, mesh=mesh, in_specs=in_specs, out_specs=out_specs, check_vma=False
    )
```

```python
import functools

import jax
import jax.numpy as jnp
from jax import lax
from jax.experimental import pallas as pl
from jax.experimental.pallas import tpu as pltpu
from jax.sharding import PartitionSpec as P

NC = 128
CYCLES = 2


finest_accuracy = lax.Precision.HIGHEST


def sweep(behind, centre, ahead, courant):
    total = None
    for value, weight in (
        (behind, lambda: courant * (1.0 + courant) * 0.5),
        (centre, lambda: 1.0 - courant * courant),
        (ahead, lambda: courant * (courant - 1.0) * 0.5),
    ):
        if value is not None:
            term = weight() * value
            total = term if total is None else total + term
    return total


def advance(stack, winds, axis):
    length = NC
    for cycle in range(CYCLES):
        stack = [
            None if line is None else sweep(
                pltpu.roll(line, 1, axis), line, pltpu.roll(line, length - 1, axis),
                winds(cycle, 0, cycle + at),
            )
            for at, line in enumerate(stack)
        ]
        stack = [
            sweep(stack[at - 1], stack[at], stack[at + 1], winds(cycle, 1, cycle + at))
            for at in range(1, len(stack) - 1)
        ]
    return stack


def select(pick, values, contract):
    pick = pick.astype(jnp.bfloat16)
    total = None
    for _ in range(3):
        part = values.astype(jnp.bfloat16)
        values = values - part.astype(jnp.float32)
        product = lax.dot_general(
            pick, part, (contract, ((), ())), preferred_element_type=jnp.float32
        )
        total = product if total is None else total + product
    return total


def forecast_kernel(
    row_total, column_total, covariance_in, courants_in, noise_in, targets_in, variance_in,
    out, gain_out, rows_out, innovation_out,
    covariance, courants, noise, targets, variance, sites, gain_all, rows_all, innovation_all,
    wind, done, travelled, term, arrived, behind, ahead, load,
    far_send, far_recv, near_send, near_recv, behind_send, behind_recv, ahead_send, ahead_recv,
    gain_send, gain_recv, rows_send, rows_recv, innovation_send, innovation_recv,
):
    row = lax.axis_index("row")
    column = lax.axis_index("col")
    height, width = covariance.shape
    band_rows, band_columns = height // NC, width // NC
    grid_rows = courants.shape[2]
    half = lax.rem(row, 2)
    partner = row + 1 - 2 * half
    far_target = lax.rem(row + 4 * half - 2 + row_total, row_total)
    far_source = lax.rem(row + 2 - 4 * half + row_total, row_total)
    before = lax.rem(column + column_total - 1, column_total)
    after = lax.rem(column + 1, column_total)
    mesh_id = pl.DeviceIdType.MESH

    loads = [
        pltpu.make_async_copy(source, target, load.at[at])
        for at, (source, target) in enumerate(
            ((covariance_in, covariance), (courants_in, courants), (noise_in, noise),
             (targets_in, targets), (variance_in, variance))
        )
    ]
    for transfer in loads:
        transfer.start()
    barrier = pltpu.get_barrier_semaphore()
    for step in range(1, column_total):
        peer = lax.rem(column + step, column_total)
        pl.semaphore_signal(barrier, 1, device_id={"col": peer}, device_id_type=mesh_id)
    for step in range(1, row_total):
        peer = lax.rem(row + step, row_total)
        pl.semaphore_signal(barrier, 1, device_id={"row": peer}, device_id_type=mesh_id)
    for transfer in loads:
        transfer.wait()
    pl.semaphore_wait(barrier, row_total + column_total - 2)

    def chunk(k):
        return covariance.at[:, k * NC : (k + 1) * NC]

    def copy(source, target, send, recv, at, axis, peer):
        return pltpu.make_async_remote_copy(
            src_ref=source, dst_ref=target, send_sem=send.at[at], recv_sem=recv.at[at],
            device_id={axis: peer}, device_id_type=mesh_id,
        )

    far = [
        copy(chunk(k), travelled.at[k], far_send, far_recv, k, "row", far_target)
        for k in range(band_columns)
    ]
    for transfer in far:
        transfer.start()

    stations = targets.shape[1]
    row_share, column_share = stations // row_total, stations // column_total
    sites[...] = jnp.broadcast_to(targets[...], (NC, stations)).T

    window = 2 * band_rows + 2 * CYCLES
    pair_first = (row - half) * band_rows - CYCLES + grid_rows
    for cycle in range(CYCLES):
        for component in range(2):
            for at in range(window):
                line = courants[
                    cycle, component, pl.ds(lax.rem(pair_first + at, grid_rows), 1), :
                ]
                wind[cycle, component, at] = jnp.broadcast_to(line, (NC, NC)).T

    def winds_of(offset):
        return lambda cycle, component, at: wind[cycle, component, offset + at]

    own_offset = half * band_rows
    other_offset = band_rows - own_offset

    def own_part(k, _):
        columns = pl.ds(pl.multiple_of(k * NC, NC), NC)
        own = [covariance[i * NC : (i + 1) * NC, columns] for i in range(band_rows)]
        lines = advance([None] * CYCLES + own + [None] * CYCLES, winds_of(own_offset), 0)
        for i, line in enumerate(lines):
            done[k, i * NC : (i + 1) * NC, :] = line
        return 0

    lax.fori_loop(0, band_columns, own_part, 0)

    def line_of(buffer, k, i):
        return buffer.at[k, i * NC : (i + 1) * NC]

    near = [
        [
            copy(line_of(term, k, i), line_of(arrived, k, i), near_send, near_recv,
                 k * band_rows + i, "row", partner)
            for i in range(band_rows)
        ]
        for k in range(band_columns)
    ]
    sides = [[] for _ in range(band_rows)]

    def finish(k):
        for i in range(band_rows):
            near[k][i].wait_recv()
            rows = slice(i * NC, (i + 1) * NC)
            done[k, rows, :] = done[k, rows, :] + arrived[k, rows, :]
            if k < CYCLES:
                transfer = copy(line_of(done, k, i), line_of(ahead, k, i), ahead_send, ahead_recv,
                                k * band_rows + i, "col", before)
                transfer.start()
                sides[i].append(transfer)
            if k >= band_columns - CYCLES:
                at = k - (band_columns - CYCLES)
                transfer = copy(line_of(done, k, i), line_of(behind, at, i), behind_send,
                                behind_recv, at * band_rows + i, "col", after)
                transfer.start()
                sides[i].append(transfer)

    for k in range(band_columns):
        far[k].wait_recv()
        lower, upper = [], []
        for i in range(band_rows):
            rows = slice(i * NC, (i + 1) * NC)
            own, other = covariance[rows, k * NC : (k + 1) * NC], travelled[k, rows, :]
            lower.append(jnp.where(half == 1, other, own))
            upper.append(jnp.where(half == 1, own, other))
        lines = advance(lower + [None] * band_rows + upper, winds_of(other_offset), 0)
        for i, line in enumerate(lines):
            term[k, i * NC : (i + 1) * NC, :] = line
            near[k][i].start()
        if k:
            finish(k - 1)
    finish(band_columns - 1)

    column_first = column * band_columns - CYCLES + grid_rows
    column_winds = {
        (cycle, component, at): courants[
            cycle, component, pl.ds(lax.rem(column_first + at, grid_rows), 1), :
        ]
        for cycle in range(CYCLES)
        for component in range(2)
        for at in range(band_columns + 2 * CYCLES)
    }
    step = 32
    for i in range(band_rows):
        for transfer in sides[i]:
            transfer.wait_recv()
        cell_noise = noise[i : i + 1, :]

        def piece(m, _):
            first = pl.multiple_of(m * step, step)
            rows = pl.ds(i * NC + first, step)
            stack = [behind[k, rows, :] for k in range(CYCLES)]
            stack += [done[k, rows, :] for k in range(band_columns)]
            stack += [ahead[k, rows, :] for k in range(CYCLES)]
            lines = advance(stack, lambda *key: column_winds[key], 1)
            matches = first + lax.broadcasted_iota(
                jnp.int32, (step, NC), 0
            ) == lax.broadcasted_iota(jnp.int32, (step, NC), 1)
            for k, line in enumerate(lines):
                here = row * band_rows + i == column * band_columns + k
                extra = jnp.where(matches & here, cell_noise, 0.0)
                out[rows, k * NC : (k + 1) * NC] = line + extra
            return 0

        lax.fori_loop(0, NC // step, piece, 0)

    def picks(share, index, extent):
        first = pl.multiple_of(index * share, share)
        local = sites[pl.ds(first, share), :] - index * extent
        lanes = lax.broadcasted_iota(jnp.int32, (share, NC), 1)
        return jnp.concatenate(
            [jnp.where(local == lanes + at, 1.0, 0.0) for at in range(0, extent, NC)], axis=1
        )

    pick_rows = picks(row_share, row, height)
    pick_columns = picks(column_share, column, width)

    def gain_block(index):
        return gain_all.at[pl.ds(pl.multiple_of(index * column_share, column_share), column_share)]

    def rows_block(index):
        return rows_all.at[pl.ds(pl.multiple_of(index * row_share, row_share), row_share)]

    def innovation_block(index):
        return innovation_all.at[pl.ds(pl.multiple_of(index * row_share, row_share), row_share)]

    gain_block(column)[...] = select(pick_columns, out[...], ((1,), (1,)))

    def exchange(block, me, axis, total, send, recv):
        copies = []
        for step in range(1, total):
            peer = lax.rem(me + step, total)
            transfer = pltpu.make_async_remote_copy(
                src_ref=block(me), dst_ref=block(me),
                send_sem=send.at[step], recv_sem=recv.at[step],
                device_id={axis: peer}, device_id_type=pl.DeviceIdType.MESH,
            )
            transfer.start()
            copies.append(transfer)
        return copies

    def arrive(block, me, axis, total, send, recv):
        for step in range(1, total):
            source = lax.rem(me - step + total, total)
            pltpu.make_async_remote_copy(
                src_ref=block(source), dst_ref=block(source),
                send_sem=send.at[step], recv_sem=recv.at[step],
                device_id={axis: source}, device_id_type=pl.DeviceIdType.MESH,
            ).wait_recv()

    sent = exchange(gain_block, column, "col", column_total, gain_send, gain_recv)
    rows_block(row)[...] = select(pick_rows, out[...], ((1,), (0,)))
    sent += exchange(rows_block, row, "row", row_total, rows_send, rows_recv)
    arrive(gain_block, column, "col", column_total, gain_send, gain_recv)
    innovation_block(row)[...] = select(pick_rows, gain_all[...], ((1,), (1,)))
    sent += exchange(innovation_block, row, "row", row_total, innovation_send, innovation_recv)
    gain_out[...] = gain_all[...]
    arrive(rows_block, row, "row", row_total, rows_send, rows_recv)
    rows_out[...] = rows_all[...]
    arrive(innovation_block, row, "row", row_total, innovation_send, innovation_recv)
    square = (stations, stations)
    diagonal = lax.broadcasted_iota(jnp.int32, square, 0) == lax.broadcasted_iota(
        jnp.int32, square, 1
    )
    innovation_out[...] = innovation_all[...] + jnp.where(diagonal, variance[...], 0.0)
    for transfer in far + sum(near + sides, []) + sent:
        transfer.wait_send()


def forecast_call(covariance, courants, noise, targets, variance, row_total, column_total):
    height, width = covariance.shape
    stations = targets.shape[0]
    band_rows, band_columns = height // NC, width // NC
    vmem = pl.BlockSpec(memory_space=pltpu.VMEM)
    lines = pltpu.VMEM((band_columns, height, NC), jnp.float32)
    side = pltpu.VMEM((CYCLES, height, NC), jnp.float32)
    window = 2 * band_rows + 2 * CYCLES
    shapes = [(stations, height), (stations, width), (stations, stations)]
    return pl.pallas_call(
        functools.partial(forecast_kernel, row_total, column_total),
        out_shape=[
            jax.ShapeDtypeStruct(shape, jnp.float32) for shape in [covariance.shape] + shapes
        ],
        in_specs=[pl.BlockSpec(memory_space=pltpu.HBM)] * 5,
        out_specs=[vmem] * 4,
        scratch_shapes=[
            pltpu.VMEM(covariance.shape, jnp.float32),
            pltpu.VMEM(courants.shape, jnp.float32),
            pltpu.VMEM(noise.shape, jnp.float32),
            pltpu.VMEM((1, stations), jnp.int32),
            pltpu.VMEM((1, stations), jnp.float32),
            pltpu.VMEM((stations, NC), jnp.int32),
        ]
        + [pltpu.VMEM(shape, jnp.float32) for shape in shapes]
        + [pltpu.VMEM((CYCLES, 2, window, NC, NC), jnp.float32)]
        + [lines] * 4
        + [side] * 2
        + [pltpu.SemaphoreType.DMA((5,))]
        + [pltpu.SemaphoreType.DMA((band_columns,))] * 2
        + [pltpu.SemaphoreType.DMA((band_columns * band_rows,))] * 2
        + [pltpu.SemaphoreType.DMA((CYCLES * band_rows,))] * 4
        + [pltpu.SemaphoreType.DMA((column_total,))] * 2
        + [pltpu.SemaphoreType.DMA((row_total,))] * 4,
        compiler_params=pltpu.CompilerParams(
            collective_id=0, has_side_effects=True, vmem_limit_bytes=40 * 2**20
        ),
    )(covariance, courants, noise, targets[None, :], variance[None, :])


PIVOTS = 4


def invert_block(d):
    def mul(x, y):
        return [[x[i][0] * y[0][j] + x[i][1] * y[1][j] for j in range(2)] for i in range(2)]

    def inv(x):
        scale = 1.0 / (x[0][0] * x[1][1] - x[0][1] * x[1][0])
        return [[x[1][1] * scale, -x[0][1] * scale], [-x[1][0] * scale, x[0][0] * scale]]

    def quarter(i, j):
        return [[d[2 * i + a][2 * j + b] for b in range(2)] for a in range(2)]

    def combine(x, y, sign):
        return [[x[i][j] + sign * y[i][j] for j in range(2)] for i in range(2)]

    e, f, g, h = quarter(0, 0), quarter(0, 1), quarter(1, 0), quarter(1, 1)
    ei = inv(e)
    eif, gei = mul(ei, f), mul(g, ei)
    si = inv(combine(h, mul(g, eif), -1.0))
    low = mul(si, gei)
    upper = mul(eif, si)
    first = combine(ei, mul(eif, low), 1.0)
    return [
        first[0] + [-upper[0][0], -upper[0][1]],
        first[1] + [-upper[1][0], -upper[1][1]],
        [-low[0][0], -low[0][1]] + si[0],
        [-low[1][0], -low[1][1]] + si[1],
    ]


def invert(matrix):
    n = matrix.shape[0]
    group = 8
    lanes = lax.broadcasted_iota(jnp.int32, (1, n), 1)
    sublanes = lax.broadcasted_iota(jnp.int32, (group, n), 0)
    parts = [matrix[i : i + group] for i in range(0, n, group)]
    for first in range(0, n, PIVOTS):
        home, at = first // group, first % group
        columns = [
            [jnp.broadcast_to(part[:, first + p : first + p + 1], (group, n)) for p in range(PIVOTS)]
            for part in parts
        ]
        block = [
            [columns[home][p][at + q : at + q + 1] for p in range(PIVOTS)] for q in range(PIVOTS)
        ]
        inverse = invert_block(block)
        outside = jnp.where((lanes >= first) & (lanes < first + PIVOTS), 0.0, 1.0)
        panel = [
            jnp.where(lanes == first + q, 1.0, parts[home][at + q : at + q + 1] * outside)
            for q in range(PIVOTS)
        ]
        solved = [
            sum(inverse[q][p] * panel[p] for p in range(1, PIVOTS)) + inverse[q][0] * panel[0]
            for q in range(PIVOTS)
        ]
        wide = [jnp.broadcast_to(row, (group, n)) for row in solved]
        updated = []
        for i, part in enumerate(parts):
            terms = [columns[i][p] * wide[p] for p in range(PIVOTS)]
            new = part * outside - ((terms[0] + terms[1]) + (terms[2] + terms[3]))
            if i == home:
                for q in range(PIVOTS):
                    new = jnp.where(sublanes == at + q, wide[q], new)
            updated.append(new)
        parts = updated
    return jnp.concatenate(parts, axis=0)


def analysis_kernel(spread, innovation, rows, gain, out):
    matrix = innovation[...]
    matrix = (matrix + matrix.T) * 0.5
    inverse = invert(matrix)
    weighted = jnp.dot(
        inverse, rows[...], precision=finest_accuracy, preferred_element_type=jnp.float32
    )
    out[...] = spread[...] - lax.dot_general(
        gain[...], weighted, (((0,), (0,)), ((), ())),
        precision=finest_accuracy, preferred_element_type=jnp.float32,
    )


def analysis_call(spread, innovation, rows, gain):
    stations = innovation.shape[0]
    if stations > NC:
        factor = jnp.linalg.cholesky(innovation)
        inverse = jax.scipy.linalg.solve_triangular(
            factor, jnp.eye(stations, dtype=jnp.float32), lower=True
        )
        left = jnp.dot(inverse, gain, precision=finest_accuracy)
        right = jnp.dot(inverse, rows, precision=finest_accuracy)
        return spread - lax.dot_general(
            left, right, (((0,), (0,)), ((), ())), precision=finest_accuracy
        )
    vmem = pl.BlockSpec(memory_space=pltpu.VMEM)
    return pl.pallas_call(
        analysis_kernel,
        out_shape=jax.ShapeDtypeStruct(spread.shape, jnp.float32),
        in_specs=[vmem] * 4,
        out_specs=vmem,
        compiler_params=pltpu.CompilerParams(vmem_limit_bytes=24 * 2**20),
    )(spread, innovation, rows, gain)


def per_device(covariance, courants, process_noise_spread, sensor_targets, noise_variance):
    spread, gain, rows, innovation = forecast_call(
        covariance, courants, process_noise_spread, sensor_targets, noise_variance,
        lax.axis_size("row"), lax.axis_size("col"),
    )
    return analysis_call(spread, innovation, rows, gain)


def solution(mesh):
    in_specs = (P("row", "col"), P(), P("row", None), P(), P())
    out_specs = P("row", "col")
    return jax.shard_map(
        per_device, mesh=mesh, in_specs=in_specs, out_specs=out_specs, check_vma=False
    )
```

```python
import functools

import jax
import jax.numpy as jnp
from jax import lax
from jax.experimental import pallas as pl
from jax.experimental.pallas import tpu as pltpu
from jax.sharding import PartitionSpec as P

NC = 128
CYCLES = 2


finest_accuracy = lax.Precision.HIGHEST


def sweep(behind, centre, ahead, courant):
    total = None
    for value, weight in (
        (behind, lambda: courant * (1.0 + courant) * 0.5),
        (centre, lambda: 1.0 - courant * courant),
        (ahead, lambda: courant * (courant - 1.0) * 0.5),
    ):
        if value is not None:
            term = weight() * value
            total = term if total is None else total + term
    return total


def advance(stack, winds, axis):
    length = NC
    for cycle in range(CYCLES):
        stack = [
            None if line is None else sweep(
                pltpu.roll(line, 1, axis), line, pltpu.roll(line, length - 1, axis),
                winds(cycle, 0, cycle + at),
            )
            for at, line in enumerate(stack)
        ]
        stack = [
            sweep(stack[at - 1], stack[at], stack[at + 1], winds(cycle, 1, cycle + at))
            for at in range(1, len(stack) - 1)
        ]
    return stack


def select(pick, values, contract):
    pick = pick.astype(jnp.bfloat16)
    total = None
    for _ in range(3):
        part = values.astype(jnp.bfloat16)
        values = values - part.astype(jnp.float32)
        product = lax.dot_general(
            pick, part, (contract, ((), ())), preferred_element_type=jnp.float32
        )
        total = product if total is None else total + product
    return total


def forecast_kernel(
    row_total, column_total, covariance_in, courants_in, noise_in, targets_in, variance_in,
    out, gain_out, rows_out, innovation_out,
    covariance, courants, noise, targets, variance, sites, gain_all, rows_all, innovation_all,
    wind, done, travelled, term, arrived, behind, ahead, load,
    far_send, far_recv, near_send, near_recv, behind_send, behind_recv, ahead_send, ahead_recv,
    gain_send, gain_recv, rows_send, rows_recv, innovation_send, innovation_recv,
):
    row = lax.axis_index("row")
    column = lax.axis_index("col")
    height, width = covariance.shape
    band_rows, band_columns = height // NC, width // NC
    grid_rows = courants.shape[2]
    half = lax.rem(row, 2)
    partner = row + 1 - 2 * half
    far_target = lax.rem(row + 4 * half - 2 + row_total, row_total)
    far_source = lax.rem(row + 2 - 4 * half + row_total, row_total)
    before = lax.rem(column + column_total - 1, column_total)
    after = lax.rem(column + 1, column_total)
    mesh_id = pl.DeviceIdType.MESH

    loads = [
        pltpu.make_async_copy(source, target, load.at[at])
        for at, (source, target) in enumerate(
            ((covariance_in, covariance), (courants_in, courants), (noise_in, noise),
             (targets_in, targets), (variance_in, variance))
        )
    ]
    for transfer in loads:
        transfer.start()
    barrier = pltpu.get_barrier_semaphore()
    for step in range(1, column_total):
        peer = lax.rem(column + step, column_total)
        pl.semaphore_signal(barrier, 1, device_id={"col": peer}, device_id_type=mesh_id)
    for step in range(1, row_total):
        peer = lax.rem(row + step, row_total)
        pl.semaphore_signal(barrier, 1, device_id={"row": peer}, device_id_type=mesh_id)
    for transfer in loads:
        transfer.wait()
    pl.semaphore_wait(barrier, row_total + column_total - 2)

    def chunk(k):
        return covariance.at[:, k * NC : (k + 1) * NC]

    def copy(source, target, send, recv, at, axis, peer):
        return pltpu.make_async_remote_copy(
            src_ref=source, dst_ref=target, send_sem=send.at[at], recv_sem=recv.at[at],
            device_id={axis: peer}, device_id_type=mesh_id,
        )

    far = [
        copy(chunk(k), travelled.at[k], far_send, far_recv, k, "row", far_target)
        for k in range(band_columns)
    ]
    for transfer in far:
        transfer.start()

    stations = targets.shape[1]
    row_share, column_share = stations // row_total, stations // column_total
    sites[...] = jnp.broadcast_to(targets[...], (NC, stations)).T

    window = 2 * band_rows + 2 * CYCLES
    pair_first = (row - half) * band_rows - CYCLES + grid_rows
    for cycle in range(CYCLES):
        for component in range(2):
            for at in range(window):
                line = courants[
                    cycle, component, pl.ds(lax.rem(pair_first + at, grid_rows), 1), :
                ]
                wind[cycle, component, at] = jnp.broadcast_to(line, (NC, NC)).T

    def winds_of(offset):
        return lambda cycle, component, at: wind[cycle, component, offset + at]

    own_offset = half * band_rows
    other_offset = band_rows - own_offset

    def own_part(k, _):
        columns = pl.ds(pl.multiple_of(k * NC, NC), NC)
        own = [covariance[i * NC : (i + 1) * NC, columns] for i in range(band_rows)]
        lines = advance([None] * CYCLES + own + [None] * CYCLES, winds_of(own_offset), 0)
        for i, line in enumerate(lines):
            done[k, i * NC : (i + 1) * NC, :] = line
        return 0

    lax.fori_loop(0, band_columns, own_part, 0)

    def line_of(buffer, k, i):
        return buffer.at[k, i * NC : (i + 1) * NC]

    near = [
        [
            copy(line_of(term, k, i), line_of(arrived, k, i), near_send, near_recv,
                 k * band_rows + i, "row", partner)
            for i in range(band_rows)
        ]
        for k in range(band_columns)
    ]
    sides = [[] for _ in range(band_rows)]

    def finish(k):
        for i in range(band_rows):
            near[k][i].wait_recv()
            rows = slice(i * NC, (i + 1) * NC)
            done[k, rows, :] = done[k, rows, :] + arrived[k, rows, :]
            if k < CYCLES:
                transfer = copy(line_of(done, k, i), line_of(ahead, k, i), ahead_send, ahead_recv,
                                k * band_rows + i, "col", before)
                transfer.start()
                sides[i].append(transfer)
            if k >= band_columns - CYCLES:
                at = k - (band_columns - CYCLES)
                transfer = copy(line_of(done, k, i), line_of(behind, at, i), behind_send,
                                behind_recv, at * band_rows + i, "col", after)
                transfer.start()
                sides[i].append(transfer)

    for k in range(band_columns):
        far[k].wait_recv()
        lower, upper = [], []
        for i in range(band_rows):
            rows = slice(i * NC, (i + 1) * NC)
            own, other = covariance[rows, k * NC : (k + 1) * NC], travelled[k, rows, :]
            lower.append(jnp.where(half == 1, other, own))
            upper.append(jnp.where(half == 1, own, other))
        lines = advance(lower + [None] * band_rows + upper, winds_of(other_offset), 0)
        for i, line in enumerate(lines):
            term[k, i * NC : (i + 1) * NC, :] = line
            near[k][i].start()
        if k:
            finish(k - 1)
    finish(band_columns - 1)

    column_first = column * band_columns - CYCLES + grid_rows
    column_winds = {
        (cycle, component, at): courants[
            cycle, component, pl.ds(lax.rem(column_first + at, grid_rows), 1), :
        ]
        for cycle in range(CYCLES)
        for component in range(2)
        for at in range(band_columns + 2 * CYCLES)
    }
    step = 32
    for i in range(band_rows):
        for transfer in sides[i]:
            transfer.wait_recv()
        cell_noise = noise[i : i + 1, :]

        def piece(m, _):
            first = pl.multiple_of(m * step, step)
            rows = pl.ds(i * NC + first, step)
            stack = [behind[k, rows, :] for k in range(CYCLES)]
            stack += [done[k, rows, :] for k in range(band_columns)]
            stack += [ahead[k, rows, :] for k in range(CYCLES)]
            lines = advance(stack, lambda *key: column_winds[key], 1)
            matches = first + lax.broadcasted_iota(
                jnp.int32, (step, NC), 0
            ) == lax.broadcasted_iota(jnp.int32, (step, NC), 1)
            for k, line in enumerate(lines):
                here = row * band_rows + i == column * band_columns + k
                extra = jnp.where(matches & here, cell_noise, 0.0)
                out[rows, k * NC : (k + 1) * NC] = line + extra
            return 0

        lax.fori_loop(0, NC // step, piece, 0)

    def picks(share, index, extent):
        first = pl.multiple_of(index * share, share)
        local = sites[pl.ds(first, share), :] - index * extent
        lanes = lax.broadcasted_iota(jnp.int32, (share, NC), 1)
        return jnp.concatenate(
            [jnp.where(local == lanes + at, 1.0, 0.0) for at in range(0, extent, NC)], axis=1
        )

    pick_rows = picks(row_share, row, height)
    pick_columns = picks(column_share, column, width)

    def gain_block(index):
        return gain_all.at[pl.ds(pl.multiple_of(index * column_share, column_share), column_share)]

    def rows_block(index):
        return rows_all.at[pl.ds(pl.multiple_of(index * row_share, row_share), row_share)]

    def innovation_block(index):
        return innovation_all.at[pl.ds(pl.multiple_of(index * row_share, row_share), row_share)]

    gain_block(column)[...] = select(pick_columns, out[...], ((1,), (1,)))

    def exchange(block, me, axis, total, send, recv):
        copies = []
        for step in range(1, total):
            peer = lax.rem(me + step, total)
            transfer = pltpu.make_async_remote_copy(
                src_ref=block(me), dst_ref=block(me),
                send_sem=send.at[step], recv_sem=recv.at[step],
                device_id={axis: peer}, device_id_type=pl.DeviceIdType.MESH,
            )
            transfer.start()
            copies.append(transfer)
        return copies

    def arrive(block, me, axis, total, send, recv):
        for step in range(1, total):
            source = lax.rem(me - step + total, total)
            pltpu.make_async_remote_copy(
                src_ref=block(source), dst_ref=block(source),
                send_sem=send.at[step], recv_sem=recv.at[step],
                device_id={axis: source}, device_id_type=pl.DeviceIdType.MESH,
            ).wait_recv()

    sent = exchange(gain_block, column, "col", column_total, gain_send, gain_recv)
    rows_block(row)[...] = select(pick_rows, out[...], ((1,), (0,)))
    sent += exchange(rows_block, row, "row", row_total, rows_send, rows_recv)
    arrive(gain_block, column, "col", column_total, gain_send, gain_recv)
    innovation_block(row)[...] = select(pick_rows, gain_all[...], ((1,), (1,)))
    sent += exchange(innovation_block, row, "row", row_total, innovation_send, innovation_recv)
    gain_out[...] = gain_all[...]
    arrive(rows_block, row, "row", row_total, rows_send, rows_recv)
    rows_out[...] = rows_all[...]
    arrive(innovation_block, row, "row", row_total, innovation_send, innovation_recv)
    square = (stations, stations)
    diagonal = lax.broadcasted_iota(jnp.int32, square, 0) == lax.broadcasted_iota(
        jnp.int32, square, 1
    )
    innovation_out[...] = innovation_all[...] + jnp.where(diagonal, variance[...], 0.0)
    for transfer in far + sum(near + sides, []) + sent:
        transfer.wait_send()


def forecast_call(covariance, courants, noise, targets, variance, row_total, column_total):
    height, width = covariance.shape
    stations = targets.shape[0]
    band_rows, band_columns = height // NC, width // NC
    vmem = pl.BlockSpec(memory_space=pltpu.VMEM)
    lines = pltpu.VMEM((band_columns, height, NC), jnp.float32)
    side = pltpu.VMEM((CYCLES, height, NC), jnp.float32)
    window = 2 * band_rows + 2 * CYCLES
    shapes = [(stations, height), (stations, width), (stations, stations)]
    return pl.pallas_call(
        functools.partial(forecast_kernel, row_total, column_total),
        out_shape=[
            jax.ShapeDtypeStruct(shape, jnp.float32) for shape in [covariance.shape] + shapes
        ],
        in_specs=[pl.BlockSpec(memory_space=pltpu.HBM)] * 5,
        out_specs=[vmem] * 4,
        scratch_shapes=[
            pltpu.VMEM(covariance.shape, jnp.float32),
            pltpu.VMEM(courants.shape, jnp.float32),
            pltpu.VMEM(noise.shape, jnp.float32),
            pltpu.VMEM((1, stations), jnp.int32),
            pltpu.VMEM((1, stations), jnp.float32),
            pltpu.VMEM((stations, NC), jnp.int32),
        ]
        + [pltpu.VMEM(shape, jnp.float32) for shape in shapes]
        + [pltpu.VMEM((CYCLES, 2, window, NC, NC), jnp.float32)]
        + [lines] * 4
        + [side] * 2
        + [pltpu.SemaphoreType.DMA((5,))]
        + [pltpu.SemaphoreType.DMA((band_columns,))] * 2
        + [pltpu.SemaphoreType.DMA((band_columns * band_rows,))] * 2
        + [pltpu.SemaphoreType.DMA((CYCLES * band_rows,))] * 4
        + [pltpu.SemaphoreType.DMA((column_total,))] * 2
        + [pltpu.SemaphoreType.DMA((row_total,))] * 4,
        compiler_params=pltpu.CompilerParams(
            collective_id=0, has_side_effects=True, vmem_limit_bytes=61 * 2**20
        ),
    )(covariance, courants, noise, targets[None, :], variance[None, :])


PIVOTS = 4


def invert_block(d):
    def mul(x, y):
        return [[x[i][0] * y[0][j] + x[i][1] * y[1][j] for j in range(2)] for i in range(2)]

    def inv(x):
        scale = 1.0 / (x[0][0] * x[1][1] - x[0][1] * x[1][0])
        return [[x[1][1] * scale, -x[0][1] * scale], [-x[1][0] * scale, x[0][0] * scale]]

    def quarter(i, j):
        return [[d[2 * i + a][2 * j + b] for b in range(2)] for a in range(2)]

    def combine(x, y, sign):
        return [[x[i][j] + sign * y[i][j] for j in range(2)] for i in range(2)]

    e, f, g, h = quarter(0, 0), quarter(0, 1), quarter(1, 0), quarter(1, 1)
    ei = inv(e)
    eif, gei = mul(ei, f), mul(g, ei)
    si = inv(combine(h, mul(g, eif), -1.0))
    low = mul(si, gei)
    upper = mul(eif, si)
    first = combine(ei, mul(eif, low), 1.0)
    return [
        first[0] + [-upper[0][0], -upper[0][1]],
        first[1] + [-upper[1][0], -upper[1][1]],
        [-low[0][0], -low[0][1]] + si[0],
        [-low[1][0], -low[1][1]] + si[1],
    ]


def invert(matrix):
    n = matrix.shape[0]
    group = 8
    lanes = lax.broadcasted_iota(jnp.int32, (1, n), 1)
    sublanes = lax.broadcasted_iota(jnp.int32, (group, n), 0)
    parts = [matrix[i : i + group] for i in range(0, n, group)]
    for first in range(0, n, PIVOTS):
        home, at = first // group, first % group
        columns = [
            [jnp.broadcast_to(part[:, first + p : first + p + 1], (group, n)) for p in range(PIVOTS)]
            for part in parts
        ]
        block = [
            [columns[home][p][at + q : at + q + 1] for p in range(PIVOTS)] for q in range(PIVOTS)
        ]
        inverse = invert_block(block)
        outside = jnp.where((lanes >= first) & (lanes < first + PIVOTS), 0.0, 1.0)
        panel = [
            jnp.where(lanes == first + q, 1.0, parts[home][at + q : at + q + 1] * outside)
            for q in range(PIVOTS)
        ]
        solved = [
            sum(inverse[q][p] * panel[p] for p in range(1, PIVOTS)) + inverse[q][0] * panel[0]
            for q in range(PIVOTS)
        ]
        wide = [jnp.broadcast_to(row, (group, n)) for row in solved]
        updated = []
        for i, part in enumerate(parts):
            terms = [columns[i][p] * wide[p] for p in range(PIVOTS)]
            new = part * outside - ((terms[0] + terms[1]) + (terms[2] + terms[3]))
            if i == home:
                for q in range(PIVOTS):
                    new = jnp.where(sublanes == at + q, wide[q], new)
            updated.append(new)
        parts = updated
    return jnp.concatenate(parts, axis=0)


def analysis_kernel(
    spread_in, innovation_in, rows_in, gain_in, out, spread, innovation, rows, gain, load
):
    loads = [
        pltpu.make_async_copy(source, target, load.at[at])
        for at, (source, target) in enumerate(
            ((innovation_in, innovation), (rows_in, rows), (gain_in, gain), (spread_in, spread))
        )
    ]
    for transfer in loads:
        transfer.start()
    loads[0].wait()
    matrix = innovation[...]
    matrix = (matrix + matrix.T) * 0.5
    inverse = invert(matrix)
    for transfer in loads[1:]:
        transfer.wait()
    weighted = jnp.dot(
        inverse, rows[...], precision=finest_accuracy, preferred_element_type=jnp.float32
    )
    out[...] = spread[...] - lax.dot_general(
        gain[...], weighted, (((0,), (0,)), ((), ())),
        precision=finest_accuracy, preferred_element_type=jnp.float32,
    )


def analysis_call(spread, innovation, rows, gain):
    stations = innovation.shape[0]
    if stations > NC:
        factor = jnp.linalg.cholesky(innovation)
        inverse = jax.scipy.linalg.solve_triangular(
            factor, jnp.eye(stations, dtype=jnp.float32), lower=True
        )
        left = jnp.dot(inverse, gain, precision=finest_accuracy)
        right = jnp.dot(inverse, rows, precision=finest_accuracy)
        return spread - lax.dot_general(
            left, right, (((0,), (0,)), ((), ())), precision=finest_accuracy
        )
    vmem = pl.BlockSpec(memory_space=pltpu.VMEM)
    return pl.pallas_call(
        analysis_kernel,
        out_shape=jax.ShapeDtypeStruct(spread.shape, jnp.float32),
        in_specs=[pl.BlockSpec(memory_space=pltpu.HBM)] * 4,
        out_specs=vmem,
        scratch_shapes=[
            pltpu.VMEM(array.shape, jnp.float32) for array in (spread, innovation, rows, gain)
        ]
        + [pltpu.SemaphoreType.DMA((4,))],
        compiler_params=pltpu.CompilerParams(vmem_limit_bytes=61 * 2**20),
    )(spread, innovation, rows, gain)


def per_device(covariance, courants, process_noise_spread, sensor_targets, noise_variance):
    spread, gain, rows, innovation = forecast_call(
        covariance, courants, process_noise_spread, sensor_targets, noise_variance,
        lax.axis_size("row"), lax.axis_size("col"),
    )
    return analysis_call(spread, innovation, rows, gain)


def solution(mesh):
    in_specs = (P("row", "col"), P(), P("row", None), P(), P())
    out_specs = P("row", "col")
    return jax.shard_map(
        per_device, mesh=mesh, in_specs=in_specs, out_specs=out_specs, check_vma=False
    )
```

```python
import functools

import jax
import jax.numpy as jnp
from jax import lax
from jax.experimental import pallas as pl
from jax.experimental.pallas import tpu as pltpu
from jax.sharding import PartitionSpec as P

NC = 128
CYCLES = 2


finest_accuracy = lax.Precision.HIGHEST


def sweep(behind, centre, ahead, courant):
    total = None
    for value, weight in (
        (behind, lambda: courant * (1.0 + courant) * 0.5),
        (centre, lambda: 1.0 - courant * courant),
        (ahead, lambda: courant * (courant - 1.0) * 0.5),
    ):
        if value is not None:
            term = weight() * value
            total = term if total is None else total + term
    return total


def advance(stack, winds, axis):
    length = NC
    for cycle in range(CYCLES):
        stack = [
            None if line is None else sweep(
                pltpu.roll(line, 1, axis), line, pltpu.roll(line, length - 1, axis),
                winds(cycle, 0, cycle + at),
            )
            for at, line in enumerate(stack)
        ]
        stack = [
            sweep(stack[at - 1], stack[at], stack[at + 1], winds(cycle, 1, cycle + at))
            for at in range(1, len(stack) - 1)
        ]
    return stack


def select(pick, values, contract):
    pick = pick.astype(jnp.bfloat16)
    total = None
    for _ in range(3):
        part = values.astype(jnp.bfloat16)
        values = values - part.astype(jnp.float32)
        product = lax.dot_general(
            pick, part, (contract, ((), ())), preferred_element_type=jnp.float32
        )
        total = product if total is None else total + product
    return total


def forecast_kernel(
    row_total, column_total, covariance_in, courants_in, noise_in, targets_in, variance_in,
    spread_out, gain_out, rows_out, innovation_out,
    out, summed, store, covariance, courants, noise, targets, variance, sites, gain_all, rows_all, innovation_all,
    wind, done, travelled, term, arrived, behind, ahead, load,
    far_send, far_recv, near_send, near_recv, behind_send, behind_recv, ahead_send, ahead_recv,
    gain_send, gain_recv, rows_send, rows_recv, innovation_send, innovation_recv,
):
    row = lax.axis_index("row")
    column = lax.axis_index("col")
    height, width = covariance.shape
    band_rows, band_columns = height // NC, width // NC
    grid_rows = courants.shape[2]
    half = lax.rem(row, 2)
    partner = row + 1 - 2 * half
    far_target = lax.rem(row + 4 * half - 2 + row_total, row_total)
    far_source = lax.rem(row + 2 - 4 * half + row_total, row_total)
    before = lax.rem(column + column_total - 1, column_total)
    after = lax.rem(column + 1, column_total)
    mesh_id = pl.DeviceIdType.MESH

    loads = [
        pltpu.make_async_copy(source, target, load.at[at])
        for at, (source, target) in enumerate(
            ((covariance_in, covariance), (courants_in, courants), (noise_in, noise),
             (targets_in, targets), (variance_in, variance))
        )
    ]
    for transfer in loads:
        transfer.start()
    barrier = pltpu.get_barrier_semaphore()
    for step in range(1, column_total):
        peer = lax.rem(column + step, column_total)
        pl.semaphore_signal(barrier, 1, device_id={"col": peer}, device_id_type=mesh_id)
    for step in range(1, row_total):
        peer = lax.rem(row + step, row_total)
        pl.semaphore_signal(barrier, 1, device_id={"row": peer}, device_id_type=mesh_id)
    for transfer in loads:
        transfer.wait()
    pl.semaphore_wait(barrier, row_total + column_total - 2)

    def chunk(k):
        return covariance.at[:, k * NC : (k + 1) * NC]

    def copy(source, target, send, recv, at, axis, peer):
        return pltpu.make_async_remote_copy(
            src_ref=source, dst_ref=target, send_sem=send.at[at], recv_sem=recv.at[at],
            device_id={axis: peer}, device_id_type=mesh_id,
        )

    far = [
        copy(chunk(k), travelled.at[k], far_send, far_recv, k, "row", far_target)
        for k in range(band_columns)
    ]
    for transfer in far:
        transfer.start()

    stations = targets.shape[1]
    row_share, column_share = stations // row_total, stations // column_total
    sites[...] = jnp.broadcast_to(targets[...], (NC, stations)).T

    window = 2 * band_rows + 2 * CYCLES
    pair_first = (row - half) * band_rows - CYCLES + grid_rows
    for cycle in range(CYCLES):
        for component in range(2):
            for at in range(window):
                line = courants[
                    cycle, component, pl.ds(lax.rem(pair_first + at, grid_rows), 1), :
                ]
                wind[cycle, component, at] = jnp.broadcast_to(line, (NC, NC)).T

    def winds_of(offset):
        return lambda cycle, component, at: wind[cycle, component, offset + at]

    own_offset = half * band_rows
    other_offset = band_rows - own_offset

    def own_part(k, _):
        columns = pl.ds(pl.multiple_of(k * NC, NC), NC)
        own = [covariance[i * NC : (i + 1) * NC, columns] for i in range(band_rows)]
        lines = advance([None] * CYCLES + own + [None] * CYCLES, winds_of(own_offset), 0)
        for i, line in enumerate(lines):
            done[k, i * NC : (i + 1) * NC, :] = line
        return 0

    lax.fori_loop(0, band_columns, own_part, 0)

    def line_of(buffer, k, i):
        return buffer.at[k, i * NC : (i + 1) * NC]

    near = [
        [
            copy(line_of(term, k, i), line_of(arrived, k, i), near_send, near_recv,
                 k * band_rows + i, "row", partner)
            for i in range(band_rows)
        ]
        for k in range(band_columns)
    ]
    sides = [[] for _ in range(band_rows)]

    def finish(k):
        for i in range(band_rows):
            near[k][i].wait_recv()
            rows = slice(i * NC, (i + 1) * NC)
            done[k, rows, :] = done[k, rows, :] + arrived[k, rows, :]
            if k < CYCLES:
                transfer = copy(line_of(done, k, i), line_of(ahead, k, i), ahead_send, ahead_recv,
                                k * band_rows + i, "col", before)
                transfer.start()
                sides[i].append(transfer)
            if k >= band_columns - CYCLES:
                at = k - (band_columns - CYCLES)
                transfer = copy(line_of(done, k, i), line_of(behind, at, i), behind_send,
                                behind_recv, at * band_rows + i, "col", after)
                transfer.start()
                sides[i].append(transfer)

    for k in range(band_columns):
        far[k].wait_recv()
        lower, upper = [], []
        for i in range(band_rows):
            rows = slice(i * NC, (i + 1) * NC)
            own, other = covariance[rows, k * NC : (k + 1) * NC], travelled[k, rows, :]
            lower.append(jnp.where(half == 1, other, own))
            upper.append(jnp.where(half == 1, own, other))
        lines = advance(lower + [None] * band_rows + upper, winds_of(other_offset), 0)
        for i, line in enumerate(lines):
            term[k, i * NC : (i + 1) * NC, :] = line
            near[k][i].start()
        if k:
            finish(k - 1)
    finish(band_columns - 1)

    column_first = column * band_columns - CYCLES + grid_rows
    column_winds = {
        (cycle, component, at): courants[
            cycle, component, pl.ds(lax.rem(column_first + at, grid_rows), 1), :
        ]
        for cycle in range(CYCLES)
        for component in range(2)
        for at in range(band_columns + 2 * CYCLES)
    }
    step = 32
    for i in range(band_rows):
        for transfer in sides[i]:
            transfer.wait_recv()
        cell_noise = noise[i : i + 1, :]

        def piece(m, _):
            first = pl.multiple_of(m * step, step)
            rows = pl.ds(i * NC + first, step)
            stack = [behind[k, rows, :] for k in range(CYCLES)]
            stack += [done[k, rows, :] for k in range(band_columns)]
            stack += [ahead[k, rows, :] for k in range(CYCLES)]
            lines = advance(stack, lambda *key: column_winds[key], 1)
            matches = first + lax.broadcasted_iota(
                jnp.int32, (step, NC), 0
            ) == lax.broadcasted_iota(jnp.int32, (step, NC), 1)
            for k, line in enumerate(lines):
                here = row * band_rows + i == column * band_columns + k
                extra = jnp.where(matches & here, cell_noise, 0.0)
                out[rows, k * NC : (k + 1) * NC] = line + extra
            return 0

        lax.fori_loop(0, NC // step, piece, 0)

    def picks(share, index, extent):
        first = pl.multiple_of(index * share, share)
        local = sites[pl.ds(first, share), :] - index * extent
        lanes = lax.broadcasted_iota(jnp.int32, (share, NC), 1)
        return jnp.concatenate(
            [jnp.where(local == lanes + at, 1.0, 0.0) for at in range(0, extent, NC)], axis=1
        )

    def keep(source, target, at):
        stores.append(pltpu.make_async_copy(source, target, store.at[at]))
        stores[-1].start()

    stores = []
    keep(out, spread_out, 0)
    pick_rows = picks(row_share, row, height)
    pick_columns = picks(column_share, column, width)

    def gain_block(index):
        return gain_all.at[pl.ds(pl.multiple_of(index * column_share, column_share), column_share)]

    def rows_block(index):
        return rows_all.at[pl.ds(pl.multiple_of(index * row_share, row_share), row_share)]

    def innovation_block(index):
        return innovation_all.at[pl.ds(pl.multiple_of(index * row_share, row_share), row_share)]

    gain_block(column)[...] = select(pick_columns, out[...], ((1,), (1,)))

    def exchange(block, me, axis, total, send, recv):
        copies = []
        for step in range(1, total):
            peer = lax.rem(me + step, total)
            transfer = pltpu.make_async_remote_copy(
                src_ref=block(me), dst_ref=block(me),
                send_sem=send.at[step], recv_sem=recv.at[step],
                device_id={axis: peer}, device_id_type=pl.DeviceIdType.MESH,
            )
            transfer.start()
            copies.append(transfer)
        return copies

    def arrive(block, me, axis, total, send, recv):
        for step in range(1, total):
            source = lax.rem(me - step + total, total)
            pltpu.make_async_remote_copy(
                src_ref=block(source), dst_ref=block(source),
                send_sem=send.at[step], recv_sem=recv.at[step],
                device_id={axis: source}, device_id_type=pl.DeviceIdType.MESH,
            ).wait_recv()

    sent = exchange(gain_block, column, "col", column_total, gain_send, gain_recv)
    rows_block(row)[...] = select(pick_rows, out[...], ((1,), (0,)))
    sent += exchange(rows_block, row, "row", row_total, rows_send, rows_recv)
    arrive(gain_block, column, "col", column_total, gain_send, gain_recv)
    innovation_block(row)[...] = select(pick_rows, gain_all[...], ((1,), (1,)))
    sent += exchange(innovation_block, row, "row", row_total, innovation_send, innovation_recv)
    keep(gain_all, gain_out, 1)
    arrive(rows_block, row, "row", row_total, rows_send, rows_recv)
    keep(rows_all, rows_out, 2)
    arrive(innovation_block, row, "row", row_total, innovation_send, innovation_recv)
    square = (stations, stations)
    diagonal = lax.broadcasted_iota(jnp.int32, square, 0) == lax.broadcasted_iota(
        jnp.int32, square, 1
    )
    summed[...] = innovation_all[...] + jnp.where(diagonal, variance[...], 0.0)
    keep(summed, innovation_out, 3)
    for transfer in stores:
        transfer.wait()
    for transfer in far + sum(near + sides, []) + sent:
        transfer.wait_send()


def forecast_call(covariance, courants, noise, targets, variance, row_total, column_total):
    height, width = covariance.shape
    stations = targets.shape[0]
    band_rows, band_columns = height // NC, width // NC
    lines = pltpu.VMEM((band_columns, height, NC), jnp.float32)
    side = pltpu.VMEM((CYCLES, height, NC), jnp.float32)
    window = 2 * band_rows + 2 * CYCLES
    shapes = [(stations, height), (stations, width), (stations, stations)]
    return pl.pallas_call(
        functools.partial(forecast_kernel, row_total, column_total),
        out_shape=[
            jax.ShapeDtypeStruct(shape, jnp.float32) for shape in [covariance.shape] + shapes
        ],
        in_specs=[pl.BlockSpec(memory_space=pltpu.HBM)] * 5,
        out_specs=[pl.BlockSpec(memory_space=pltpu.HBM)] * 4,
        scratch_shapes=[
            pltpu.VMEM(covariance.shape, jnp.float32),
            pltpu.VMEM((stations, stations), jnp.float32),
            pltpu.SemaphoreType.DMA((4,)),
            pltpu.VMEM(covariance.shape, jnp.float32),
            pltpu.VMEM(courants.shape, jnp.float32),
            pltpu.VMEM(noise.shape, jnp.float32),
            pltpu.VMEM((1, stations), jnp.int32),
            pltpu.VMEM((1, stations), jnp.float32),
            pltpu.VMEM((stations, NC), jnp.int32),
        ]
        + [pltpu.VMEM(shape, jnp.float32) for shape in shapes]
        + [pltpu.VMEM((CYCLES, 2, window, NC, NC), jnp.float32)]
        + [lines] * 4
        + [side] * 2
        + [pltpu.SemaphoreType.DMA((5,))]
        + [pltpu.SemaphoreType.DMA((band_columns,))] * 2
        + [pltpu.SemaphoreType.DMA((band_columns * band_rows,))] * 2
        + [pltpu.SemaphoreType.DMA((CYCLES * band_rows,))] * 4
        + [pltpu.SemaphoreType.DMA((column_total,))] * 2
        + [pltpu.SemaphoreType.DMA((row_total,))] * 4,
        compiler_params=pltpu.CompilerParams(
            collective_id=0, has_side_effects=True, vmem_limit_bytes=61 * 2**20
        ),
    )(covariance, courants, noise, targets[None, :], variance[None, :])


PIVOTS = 4


def invert_block(d):
    def mul(x, y):
        return [[x[i][0] * y[0][j] + x[i][1] * y[1][j] for j in range(2)] for i in range(2)]

    def inv(x):
        scale = 1.0 / (x[0][0] * x[1][1] - x[0][1] * x[1][0])
        return [[x[1][1] * scale, -x[0][1] * scale], [-x[1][0] * scale, x[0][0] * scale]]

    def quarter(i, j):
        return [[d[2 * i + a][2 * j + b] for b in range(2)] for a in range(2)]

    def combine(x, y, sign):
        return [[x[i][j] + sign * y[i][j] for j in range(2)] for i in range(2)]

    e, f, g, h = quarter(0, 0), quarter(0, 1), quarter(1, 0), quarter(1, 1)
    ei = inv(e)
    eif, gei = mul(ei, f), mul(g, ei)
    si = inv(combine(h, mul(g, eif), -1.0))
    low = mul(si, gei)
    upper = mul(eif, si)
    first = combine(ei, mul(eif, low), 1.0)
    return [
        first[0] + [-upper[0][0], -upper[0][1]],
        first[1] + [-upper[1][0], -upper[1][1]],
        [-low[0][0], -low[0][1]] + si[0],
        [-low[1][0], -low[1][1]] + si[1],
    ]


def invert(matrix):
    n = matrix.shape[0]
    group = 8
    lanes = lax.broadcasted_iota(jnp.int32, (1, n), 1)
    sublanes = lax.broadcasted_iota(jnp.int32, (group, n), 0)
    parts = [matrix[i : i + group] for i in range(0, n, group)]
    for first in range(0, n, PIVOTS):
        home, at = first // group, first % group
        columns = [
            [jnp.broadcast_to(part[:, first + p : first + p + 1], (group, n)) for p in range(PIVOTS)]
            for part in parts
        ]
        block = [
            [columns[home][p][at + q : at + q + 1] for p in range(PIVOTS)] for q in range(PIVOTS)
        ]
        inverse = invert_block(block)
        outside = jnp.where((lanes >= first) & (lanes < first + PIVOTS), 0.0, 1.0)
        panel = [
            jnp.where(lanes == first + q, 1.0, parts[home][at + q : at + q + 1] * outside)
            for q in range(PIVOTS)
        ]
        solved = [
            sum(inverse[q][p] * panel[p] for p in range(1, PIVOTS)) + inverse[q][0] * panel[0]
            for q in range(PIVOTS)
        ]
        wide = [jnp.broadcast_to(row, (group, n)) for row in solved]
        updated = []
        for i, part in enumerate(parts):
            terms = [columns[i][p] * wide[p] for p in range(PIVOTS)]
            new = part * outside - ((terms[0] + terms[1]) + (terms[2] + terms[3]))
            if i == home:
                for q in range(PIVOTS):
                    new = jnp.where(sublanes == at + q, wide[q], new)
            updated.append(new)
        parts = updated
    return jnp.concatenate(parts, axis=0)


def analysis_kernel(
    spread_in, innovation_in, rows_in, gain_in, out, spread, innovation, rows, gain, load
):
    loads = [
        pltpu.make_async_copy(source, target, load.at[at])
        for at, (source, target) in enumerate(
            ((innovation_in, innovation), (rows_in, rows), (gain_in, gain), (spread_in, spread))
        )
    ]
    for transfer in loads:
        transfer.start()
    loads[0].wait()
    matrix = innovation[...]
    matrix = (matrix + matrix.T) * 0.5
    inverse = invert(matrix)
    for transfer in loads[1:]:
        transfer.wait()
    weighted = jnp.dot(
        inverse, rows[...], precision=finest_accuracy, preferred_element_type=jnp.float32
    )
    out[...] = spread[...] - lax.dot_general(
        gain[...], weighted, (((0,), (0,)), ((), ())),
        precision=finest_accuracy, preferred_element_type=jnp.float32,
    )


def analysis_call(spread, innovation, rows, gain):
    stations = innovation.shape[0]
    if stations > NC:
        factor = jnp.linalg.cholesky(innovation)
        inverse = jax.scipy.linalg.solve_triangular(
            factor, jnp.eye(stations, dtype=jnp.float32), lower=True
        )
        left = jnp.dot(inverse, gain, precision=finest_accuracy)
        right = jnp.dot(inverse, rows, precision=finest_accuracy)
        return spread - lax.dot_general(
            left, right, (((0,), (0,)), ((), ())), precision=finest_accuracy
        )
    vmem = pl.BlockSpec(memory_space=pltpu.VMEM)
    return pl.pallas_call(
        analysis_kernel,
        out_shape=jax.ShapeDtypeStruct(spread.shape, jnp.float32),
        in_specs=[pl.BlockSpec(memory_space=pltpu.HBM)] * 4,
        out_specs=vmem,
        scratch_shapes=[
            pltpu.VMEM(array.shape, jnp.float32) for array in (spread, innovation, rows, gain)
        ]
        + [pltpu.SemaphoreType.DMA((4,))],
        compiler_params=pltpu.CompilerParams(vmem_limit_bytes=61 * 2**20),
    )(spread, innovation, rows, gain)


def per_device(covariance, courants, process_noise_spread, sensor_targets, noise_variance):
    spread, gain, rows, innovation = forecast_call(
        covariance, courants, process_noise_spread, sensor_targets, noise_variance,
        lax.axis_size("row"), lax.axis_size("col"),
    )
    return analysis_call(spread, innovation, rows, gain)


def solution(mesh):
    in_specs = (P("row", "col"), P(), P("row", None), P(), P())
    out_specs = P("row", "col")
    return jax.shard_map(
        per_device, mesh=mesh, in_specs=in_specs, out_specs=out_specs, check_vma=False
    )
```
